256 devices in a mesh: cplx: 2 (over core), node: 4 (over y), edge: 32 (over z, x).
Axes of the slice: x: 4, y: 4, z: 8, core: 2. Of those that a mesh axis runs over, the one named last changes fastest.
Arguments:
- node_in: bfloat16 [16384, 512], P(('cplx', 'node', 'edge')), parts along dimension 0, may hold values from -6 to 6
- edge_in: bfloat16 [16384, 64, 128], P(('cplx', 'node', 'edge')), parts along dimension 0, may hold values from -6 to 6
- neighbours: int32 [16384, 64], P(('cplx', 'node', 'edge')), parts along dimension 0, may hold values from 0 to 8191
- edge_mask: int32 [16384, 64], P(('cplx', 'node', 'edge')), parts along dimension 0, may hold values 0 or 1
- w_src: bfloat16 [512, 128], replicated, may hold values from -0.25 to 0.25
- w_dst: bfloat16 [512, 128], replicated, may hold values from -0.25 to 0.25
- w_edge_one: bfloat16 [128, 128], replicated, may hold values from -0.5 to 0.5
- w_edge_two: bfloat16 [128, 128], replicated, may hold values from -0.5 to 0.5
- w_edge_three: bfloat16 [128, 128], replicated, may hold values from -0.5 to 0.5
- w_node: bfloat16 [128, 512], replicated, may hold values from -0.5 to 0.5
- node_cot: bfloat16 [16384, 512], P(('cplx', 'node', 'edge')), parts along dimension 0, may hold values from -6 to 6
- edge_cot: bfloat16 [16384, 64, 128], P(('cplx', 'node', 'edge')), parts along dimension 0, may hold values from -6 to 6
Outputs:
- node_out: bfloat16 [16384, 512], P(('cplx', 'node', 'edge')), parts along dimension 0
- edge_out: bfloat16 [16384, 64, 128], P(('cplx', 'node', 'edge')), parts along dimension 0
- grad_node: bfloat16 [16384, 512], P(('cplx', 'node', 'edge')), parts along dimension 0
- grad_edge: bfloat16 [16384, 64, 128], P(('cplx', 'node', 'edge')), parts along dimension 0
- grad_w_src: float32 [1024, 128], P('cplx'), parts along dimension 0
- grad_w_dst: float32 [1024, 128], P('cplx'), parts along dimension 0
- grad_w_edge_one: float32 [256, 128], P('cplx'), parts along dimension 0
- grad_w_edge_two: float32 [256, 128], P('cplx'), parts along dimension 0
- grad_w_edge_three: float32 [256, 128], P('cplx'), parts along dimension 0
- grad_w_node: float32 [256, 512], P('cplx'), parts along dimension 0
The draws below stay inside these ranges and needn't reach their ends.
There are 2 independent parts, one for each index of `cplx`. The reference program is written for one: setup_inputs(seed, part) draws one part's arguments, and reference() takes and returns one part's arrays. A program takes and returns all parts, laid end to end along the dimension named above; an argument that names none is the same for every part. Nothing has to cross between parts.
All inputs are finite; a program needn't handle non-finite values. No bound on the sum of `edge_mask` on one device may be relied on, other than what follows from the above.
Results may differ from the reference program's by a relative error of at most 0.015.
Values may be sent and summed in bfloat16 or wider, within the bound.
No kernel may reach another device: no remote copies, remote signals or barrier semaphores. Data moves between devices by JAX's collectives and lax.ppermute only.
A program may use at most 64 MiB of HBM per device.

```python
import math
import jax
import jax.numpy as jnp
from jax import lax

D = 512
DE = 128
K = 64
NRES = 8192


def set_ends(drawn, own_key, least, largest):
    dims = drawn.shape
    place = [jax.random.randint(jax.random.fold_in(own_key, axis), (), 0, dims[axis]) for axis in range(len(dims))]
    drawn = drawn.at[tuple(place)].set(least)
    longest = dims.index(max(dims))
    place[longest] = (place[longest] + 1) % dims[longest]
    return drawn.at[tuple(place)].set(largest)


def steps_of(own_key, shape, pieces, smallest, top_value):
    def one(axis_at, parts):
        steps = jax.random.uniform(jax.random.fold_in(jax.random.fold_in(own_key, 6), axis_at), (parts,), jnp.float32, smallest / len(pieces), top_value / len(pieces))
        return jnp.repeat(jnp.exp(steps), shape[axis_at] // parts).reshape((-1,) + (1,) * (len(shape) - axis_at - 1))

    level = one(*pieces[0])
    for cut in pieces[1:]:
        level = level * one(*cut)
    return level


def centred(rng, extent, scale, bound, cuts=(), kind=jnp.bfloat16):
    values = jax.random.normal(rng, extent, jnp.float32) * scale
    if len(cuts) > 0:
        values = steps_of(rng, extent, cuts, -0.22, 0.18) * values
    return jnp.clip(values, min=-bound, max=bound).astype(kind)


def setup_inputs(seed: int = 0, part: int = 0) -> dict:
    streams_of = jax.random.split(jax.random.key(seed), 13)
    part_splits = jax.random.split(jax.random.fold_in(streams_of[12], part), 13)
    node_in = centred(part_splits[0], (NRES, D), 1.0, 6.0, ((0, 128),))
    edge_in = centred(part_splits[1], (NRES, K, DE), 1.0, 6.0, ((0, 128),))
    neighbours = set_ends(jax.random.randint(part_splits[2], (NRES, K), 0, NRES), jax.random.fold_in(part_splits[2], 1), 0, NRES - 1).astype(jnp.int32)
    edge_mask = set_ends((jax.random.randint(part_splits[3], (NRES, K), 0, 4) < 3).astype(jnp.int32), jax.random.fold_in(part_splits[3], 1), 0, 1)
    w_src = centred(streams_of[4], (D, DE), D ** -0.5, 0.25)
    w_dst = centred(streams_of[5], (D, DE), D ** -0.5, 0.25)
    w_edge_one = centred(streams_of[6], (DE, DE), DE ** -0.5, 0.5)
    w_edge_two = centred(streams_of[7], (DE, DE), DE ** -0.5, 0.5)
    w_edge_three = centred(streams_of[8], (DE, DE), DE ** -0.5, 0.5)
    w_node = centred(streams_of[9], (DE, D), DE ** -0.5, 0.5)
    node_cot = centred(part_splits[10], (NRES, D), 1.0, 6.0, ((0, 128),))
    edge_cot = centred(part_splits[11], (NRES, K, DE), 1.0, 6.0, ((0, 128),))
    return dict(node_in=node_in, edge_in=edge_in, neighbours=neighbours, edge_mask=edge_mask, w_src=w_src, w_dst=w_dst, w_edge_one=w_edge_one, w_edge_two=w_edge_two, w_edge_three=w_edge_three, w_node=w_node, node_cot=node_cot, edge_cot=edge_cot)


def silu_parts(value):
    sigma_val = jax.nn.sigmoid(value)
    return (value * sigma_val, sigma_val * (1.0 + value * (1.0 - sigma_val)))

def reference(node_in, edge_in, neighbours, edge_mask, w_src, w_dst, w_edge_one, w_edge_two, w_edge_three, w_node, node_cot, edge_cot):
    total, nbr_count, edge_width = edge_in.shape
    agg_scale = 1.0 / math.sqrt(nbr_count)
    src_proj = jnp.dot(node_in, w_src, preferred_element_type=jnp.float32).astype(jnp.bfloat16)
    dst_proj = jnp.dot(node_in, w_dst, preferred_element_type=jnp.float32).astype(jnp.bfloat16)
    flat_nbr = neighbours.reshape(-1).astype(jnp.int32)
    pulled = jnp.take(dst_proj, flat_nbr, axis=0).reshape(total, nbr_count, edge_width)
    flat_edges = edge_in.reshape(total * nbr_count, edge_width)
    masked = edge_mask.astype(jnp.float32)[:, :, None]
    pre_one = jnp.dot(flat_edges, w_edge_one, preferred_element_type=jnp.float32).reshape(total, nbr_count, edge_width)
    pre_one = (pre_one + src_proj[:, None, :].astype(jnp.float32) + pulled.astype(jnp.float32)).reshape(-1, edge_width)
    act_one_f, deriv_one = silu_parts(pre_one)
    act_one = act_one_f.astype(jnp.bfloat16)
    pre_two = jnp.dot(act_one, w_edge_two, preferred_element_type=jnp.float32)
    act_two_f, deriv_two = silu_parts(pre_two)
    act_two = act_two_f.astype(jnp.bfloat16)
    update = jnp.dot(act_two, w_edge_three, preferred_element_type=jnp.float32).reshape(total, nbr_count, edge_width)
    edge_new = edge_in.astype(jnp.float32) + masked * update
    edge_out = edge_new.astype(jnp.bfloat16)
    aggregate = (lax.optimization_barrier(jnp.sum(masked * edge_new, axis=1)) * agg_scale).astype(jnp.bfloat16)
    node_out = (node_in.astype(jnp.float32) + jnp.dot(aggregate, w_node, preferred_element_type=jnp.float32)).astype(jnp.bfloat16)
    grad_agg = jnp.dot(node_cot, w_node.T, preferred_element_type=jnp.float32)
    grad_new = edge_cot.astype(jnp.float32) + masked * grad_agg[:, None, :] * agg_scale
    grad_upd = (masked * grad_new).astype(jnp.bfloat16).reshape(-1, edge_width)
    grad_pre_two = (jnp.dot(grad_upd, w_edge_three.T, preferred_element_type=jnp.float32) * deriv_two).astype(jnp.bfloat16)
    grad_pre_one = (jnp.dot(grad_pre_two, w_edge_two.T, preferred_element_type=jnp.float32) * deriv_one).astype(jnp.bfloat16)
    back_edge = jnp.dot(grad_pre_one, w_edge_one.T, preferred_element_type=jnp.float32).reshape(total, nbr_count, edge_width)
    grad_edge = (grad_new + back_edge).astype(jnp.bfloat16)
    grad_src = lax.optimization_barrier(jnp.sum(grad_pre_one.reshape(total, nbr_count, edge_width).astype(jnp.float32), axis=1)).astype(jnp.bfloat16)
    grad_dst = jnp.zeros((total, edge_width), jnp.float32).at[flat_nbr].add(grad_pre_one.astype(jnp.float32)).astype(jnp.bfloat16)
    grad_node = node_cot.astype(jnp.float32) + jnp.dot(grad_src, w_src.T, preferred_element_type=jnp.float32)
    grad_node = (grad_node + jnp.dot(grad_dst, w_dst.T, preferred_element_type=jnp.float32)).astype(jnp.bfloat16)
    node_scale = 1.0 / math.sqrt(total)
    edge_scale = 1.0 / math.sqrt(total * nbr_count)
    grad_w_src = jnp.dot(node_in.T, grad_src, preferred_element_type=jnp.float32) * node_scale
    grad_w_dst = jnp.dot(node_in.T, grad_dst, preferred_element_type=jnp.float32) * node_scale
    grad_w_node = jnp.dot(aggregate.T, node_cot, preferred_element_type=jnp.float32) * node_scale
    grad_w_one = jnp.dot(flat_edges.T, grad_pre_one, preferred_element_type=jnp.float32) * edge_scale
    grad_w_two = jnp.dot(act_one.T, grad_pre_two, preferred_element_type=jnp.float32) * edge_scale
    grad_w_three = jnp.dot(act_two.T, grad_upd, preferred_element_type=jnp.float32) * edge_scale
    return (node_out, edge_out, grad_node, grad_edge, grad_w_src, grad_w_dst, grad_w_one, grad_w_two, grad_w_three, grad_w_node)
```

```python
import math

import jax
import jax.numpy as jnp
from jax import lax
from jax.sharding import Mesh
from jax.sharding import PartitionSpec as P

RING = "z"
PLANE = ("y", "x")
ALL = ("y", "z", "x")


def exchange(value, axes):
    return lax.all_to_all(value, axes, 0, 0, tiled=True)


def gather_rows(rows):
    count, width = rows.shape
    long = lax.axis_size(RING)
    plane = lax.axis_size("y"), lax.axis_size("x")
    column = exchange(jnp.broadcast_to(rows[None], (long, count, width)), RING)
    whole = exchange(jnp.broadcast_to(column[None], (plane[0] * plane[1], *column.shape)), PLANE)
    whole = whole.reshape(plane[0], plane[1], long, count, width)
    return whole.transpose(0, 2, 1, 3, 4).reshape(-1, width)


def scatter_rows(partial):
    long = lax.axis_size(RING)
    plane = lax.axis_size("y"), lax.axis_size("x")
    width = partial.shape[-1]
    blocks = partial.astype(jnp.bfloat16).reshape(plane[0], long, plane[1], -1, width)
    blocks = blocks.transpose(0, 2, 1, 3, 4).reshape(plane[0] * plane[1], -1, width)
    summed = jnp.sum(exchange(blocks, PLANE).astype(jnp.float32), axis=0)
    summed = summed.astype(jnp.bfloat16).reshape(long, -1, width)
    return jnp.sum(exchange(summed, RING).astype(jnp.float32), axis=0)


def sum_everywhere(value, parts):
    rows, width = value.shape
    height = -(-rows // (parts * 16)) * 16
    value = jnp.pad(value.astype(jnp.bfloat16), ((0, parts * height - rows), (0, 0)))
    own = jnp.sum(exchange(value.reshape(parts, height, width), ALL).astype(jnp.float32), axis=0)
    own = jnp.broadcast_to(own.astype(jnp.bfloat16)[None], (parts, height, width))
    return exchange(own, ALL).reshape(-1, width)[:rows].astype(jnp.float32)


def silu_parts(value):
    sigma_val = jax.nn.sigmoid(value)
    return (value * sigma_val, sigma_val * (1.0 + value * (1.0 - sigma_val)))


def shards(
    node_in,
    edge_in,
    neighbours,
    edge_mask,
    w_src,
    w_dst,
    w_edge_one,
    w_edge_two,
    w_edge_three,
    w_node,
    node_cot,
    edge_cot,
):
    row_count, nbr_count, edge_width = edge_in.shape
    agg_scale = 1.0 / math.sqrt(nbr_count)
    src_proj = jnp.dot(node_in, w_src, preferred_element_type=jnp.float32).astype(jnp.bfloat16)
    targets = gather_rows(
        jnp.dot(node_in, w_dst, preferred_element_type=jnp.float32).astype(jnp.bfloat16)
    )
    total = targets.shape[0]
    node_scale = 1.0 / math.sqrt(total)
    edge_scale = 1.0 / math.sqrt(total * nbr_count)
    flat_nbr = neighbours.reshape(-1)
    pulled = jnp.take(targets, flat_nbr, axis=0).reshape(row_count, nbr_count, edge_width)
    flat_edges = edge_in.reshape(row_count * nbr_count, edge_width)
    masked = edge_mask.astype(jnp.float32)[:, :, None]
    pre_one = jnp.dot(flat_edges, w_edge_one, preferred_element_type=jnp.float32).reshape(
        row_count, nbr_count, edge_width
    )
    pre_one = (
        pre_one + src_proj[:, None, :].astype(jnp.float32) + pulled.astype(jnp.float32)
    ).reshape(-1, edge_width)
    act_one_f, deriv_one = silu_parts(pre_one)
    act_one = act_one_f.astype(jnp.bfloat16)
    pre_two = jnp.dot(act_one, w_edge_two, preferred_element_type=jnp.float32)
    act_two_f, deriv_two = silu_parts(pre_two)
    act_two = act_two_f.astype(jnp.bfloat16)
    update = jnp.dot(act_two, w_edge_three, preferred_element_type=jnp.float32).reshape(
        row_count, nbr_count, edge_width
    )
    edge_new = edge_in.astype(jnp.float32) + masked * update
    edge_out = edge_new.astype(jnp.bfloat16)
    aggregate = (jnp.sum(masked * edge_new, axis=1) * agg_scale).astype(jnp.bfloat16)
    node_out = (
        node_in.astype(jnp.float32) + jnp.dot(aggregate, w_node, preferred_element_type=jnp.float32)
    ).astype(jnp.bfloat16)
    node_term = jnp.dot(aggregate.T, node_cot, preferred_element_type=jnp.float32)
    grad_agg = jnp.dot(node_cot, w_node.T, preferred_element_type=jnp.float32)
    grad_new = edge_cot.astype(jnp.float32) + masked * grad_agg[:, None, :] * agg_scale
    grad_upd = (masked * grad_new).astype(jnp.bfloat16).reshape(-1, edge_width)
    grad_pre_two = (
        jnp.dot(grad_upd, w_edge_three.T, preferred_element_type=jnp.float32) * deriv_two
    ).astype(jnp.bfloat16)
    grad_pre_one = (
        jnp.dot(grad_pre_two, w_edge_two.T, preferred_element_type=jnp.float32) * deriv_one
    ).astype(jnp.bfloat16)
    accumulated = (
        jnp.zeros((total, edge_width), jnp.float32)
        .at[flat_nbr]
        .add(grad_pre_one.astype(jnp.float32))
    )
    grad_dst = scatter_rows(accumulated).astype(jnp.bfloat16)
    back_edge = jnp.dot(grad_pre_one, w_edge_one.T, preferred_element_type=jnp.float32).reshape(
        row_count, nbr_count, edge_width
    )
    grad_edge = (grad_new + back_edge).astype(jnp.bfloat16)
    grad_src = jnp.sum(
        grad_pre_one.reshape(row_count, nbr_count, edge_width).astype(jnp.float32), axis=1
    ).astype(jnp.bfloat16)
    term_one = jnp.dot(flat_edges.T, grad_pre_one, preferred_element_type=jnp.float32)
    term_two = jnp.dot(act_one.T, grad_pre_two, preferred_element_type=jnp.float32)
    term_three = jnp.dot(act_two.T, grad_upd, preferred_element_type=jnp.float32)
    term_src = jnp.dot(node_in.T, grad_src, preferred_element_type=jnp.float32)
    term_dst = jnp.dot(node_in.T, grad_dst, preferred_element_type=jnp.float32)
    grad_node = node_cot.astype(jnp.float32) + jnp.dot(
        grad_src, w_src.T, preferred_element_type=jnp.float32
    )
    grad_node = (grad_node + jnp.dot(grad_dst, w_dst.T, preferred_element_type=jnp.float32)).astype(
        jnp.bfloat16
    )
    terms = (term_src, term_dst, term_one, term_two, term_three, node_term.reshape(-1, edge_width))
    sums = sum_everywhere(jnp.concatenate(terms, axis=0), total // row_count)
    starts = [0]
    for term in terms:
        starts.append(starts[-1] + term.shape[0])
    sum_src, sum_dst, sum_one, sum_two, sum_three, grad_w_node = (
        sums[low:high] for low, high in zip(starts[:-1], starts[1:])
    )
    grad_w_node = grad_w_node.reshape(node_term.shape)
    return (
        node_out,
        edge_out,
        grad_node,
        grad_edge,
        sum_src * node_scale,
        sum_dst * node_scale,
        sum_one * edge_scale,
        sum_two * edge_scale,
        sum_three * edge_scale,
        grad_w_node * node_scale,
    )


def solution(mesh):
    shape = mesh.shape
    outer = shape["node"]
    inner = outer
    devices = mesh.devices.reshape(shape["cplx"], outer, shape["edge"] // inner, inner)
    mesh = Mesh(devices, ("cplx", *ALL))
    in_specs = (
        P(("cplx", *ALL), None),
        P(("cplx", *ALL), None, None),
        P(("cplx", *ALL), None),
        P(("cplx", *ALL), None),
        P(),
        P(),
        P(),
        P(),
        P(),
        P(),
        P(("cplx", *ALL), None),
        P(("cplx", *ALL), None, None),
    )
    out_specs = (
        P(("cplx", *ALL), None),
        P(("cplx", *ALL), None, None),
        P(("cplx", *ALL), None),
        P(("cplx", *ALL), None, None),
        P("cplx", None),
        P("cplx", None),
        P("cplx", None),
        P("cplx", None),
        P("cplx", None),
        P("cplx", None),
    )
    return jax.shard_map(shards, mesh=mesh, in_specs=in_specs, out_specs=out_specs, check_vma=False)
```

```python
import functools
import math

import jax
import jax.numpy as jnp
from jax import lax
from jax.experimental import pallas as pl
from jax.experimental.pallas import tpu as pltpu
from jax.sharding import Mesh
from jax.sharding import PartitionSpec as P

RING = "z"
PLANE = ("y", "x")
ALL = ("y", "z", "x")
SUMS = 4
UNROLL = 32
BLOCK = 512
PIECE = 512


def exchange(value, axes):
    return lax.all_to_all(value, axes, 0, 0, tiled=True)


def spread(value, axes):
    count = math.prod(lax.axis_size(axis) for axis in axes)
    return exchange(jnp.broadcast_to(value[None], (count, *value.shape)), axes)


def sum_first(value):
    return jnp.sum(value.astype(jnp.float32), axis=0)


def deriv(value, sigma_val):
    return sigma_val * (1.0 + value * (1.0 - sigma_val))


def edge_chain_body(
    place_ref,
    table_ref,
    base_ref,
    up_ref,
    weight_ref,
    act_one_ref,
    act_two_ref,
    grad_two_ref,
    grad_one_ref,
    total_ref,
    table,
    pulled,
    grads,
    *sums,
):
    step = pl.program_id(0)
    block = pulled.shape[0]
    count, width = table.shape

    @pl.when(step == 0)
    def _():
        def fill(at, carry):
            rows = pl.ds(pl.multiple_of(at * PIECE, PIECE), PIECE)
            table[rows, :] = table_ref[rows, :].astype(jnp.float32)
            for one in sums:
                one[rows, :] = jnp.zeros((PIECE, width), jnp.float32)
            return carry

        lax.fori_loop(0, count // PIECE, fill, 0)

    first = step * block

    def pull(at, carry):
        low = at * UNROLL
        for k in range(UNROLL):
            place = place_ref[first + low + k]
            pulled[pl.ds(low + k, 1), :] = table[pl.ds(place, 1), :]
        return carry

    lax.fori_loop(0, block // UNROLL, pull, 0)

    pre_one = base_ref[...] + pulled[...]
    sigma_one = jax.nn.sigmoid(pre_one)
    act_one = (pre_one * sigma_one).astype(jnp.bfloat16)
    act_one_ref[...] = act_one
    pre_two = jnp.dot(act_one, weight_ref[...], preferred_element_type=jnp.float32)
    sigma_two = jax.nn.sigmoid(pre_two)
    act_two_ref[...] = (pre_two * sigma_two).astype(jnp.bfloat16)
    grad_two = (up_ref[...] * deriv(pre_two, sigma_two)).astype(jnp.bfloat16)
    grad_two_ref[...] = grad_two
    back = lax.dot_general(
        grad_two,
        weight_ref[...],
        (((1,), (1,)), ((), ())),
        preferred_element_type=jnp.float32,
    )
    grad_one = (back * deriv(pre_one, sigma_one)).astype(jnp.bfloat16)
    grad_one_ref[...] = grad_one
    grads[...] = grad_one.astype(jnp.float32)

    def push(at, carry):
        low = at * UNROLL
        for k in range(UNROLL):
            one = sums[k % SUMS]
            row = pl.ds(place_ref[first + low + k], 1)
            one[row, :] += grads[pl.ds(low + k, 1), :]
        return carry

    lax.fori_loop(0, block // UNROLL, push, 0)

    @pl.when(step == pl.num_programs(0) - 1)
    def _():
        def merge(at, carry):
            rows = pl.ds(pl.multiple_of(at * PIECE, PIECE), PIECE)
            value = sums[0][rows, :]
            for one in sums[1:]:
                value = value + one[rows, :]
            total_ref[rows, :] = value.astype(jnp.bfloat16)
            return carry

        lax.fori_loop(0, count // PIECE, merge, 0)


def edge_chain(places, table, base, up, weight):
    count, width = table.shape
    edges = places.shape[0]
    rows = pl.BlockSpec((BLOCK, width), lambda i, places: (i, 0))

    def whole(shape):
        return pl.BlockSpec(shape, lambda i, places: (0, 0))

    held = pltpu.VMEM((count, width), jnp.float32)
    part = pltpu.VMEM((BLOCK, width), jnp.float32)
    return pl.pallas_call(
        edge_chain_body,
        grid_spec=pltpu.PrefetchScalarGridSpec(
            num_scalar_prefetch=1,
            grid=(edges // BLOCK,),
            in_specs=[whole((count, width)), rows, rows, whole((width, width))],
            out_specs=[rows, rows, rows, rows, whole((count, width))],
            scratch_shapes=[held, part, part] + [held] * SUMS,
        ),
        out_shape=[jax.ShapeDtypeStruct((edges, width), jnp.bfloat16)] * 4
        + [jax.ShapeDtypeStruct((count, width), jnp.bfloat16)],
        compiler_params=pltpu.CompilerParams(vmem_limit_bytes=40 * 1024 * 1024),
        cost_estimate=pl.CostEstimate(
            flops=20 * edges * width * width, bytes_accessed=60 * 2**20, transcendentals=0
        ),
        name="edge_chain",
    )(places, table, base, up, weight)


def shards(
    node_in,
    edge_in,
    neighbours,
    edge_mask,
    w_src,
    w_dst,
    w_edge_one,
    w_edge_two,
    w_edge_three,
    w_node,
    node_cot,
    edge_cot,
):
    row_count, nbr_count, edge_width = edge_in.shape
    bf16, f32 = jnp.bfloat16, jnp.float32
    dot = functools.partial(jnp.dot, preferred_element_type=f32)
    long, deep, wide = lax.axis_size(RING), lax.axis_size("y"), lax.axis_size("x")
    parts = long * deep * wide
    total = parts * row_count
    agg_scale = 1.0 / math.sqrt(nbr_count)
    node_scale = 1.0 / math.sqrt(total)
    edge_scale = 1.0 / math.sqrt(total * nbr_count)

    column = spread(dot(node_in, w_dst).astype(bf16), (RING,)).reshape(-1, edge_width)
    table = spread(column, PLANE).reshape(total, edge_width)
    own_row, rest = neighbours % row_count, neighbours // row_count
    at_x, rest = rest % wide, rest // wide
    at_z, at_y = rest % long, rest // long
    places = (((at_y * wide + at_x) * long + at_z) * row_count + own_row).reshape(-1)

    src_proj = dot(node_in, w_src).astype(bf16)
    flat_edges = edge_in.reshape(row_count * nbr_count, edge_width)
    masked = edge_mask.astype(f32)[:, :, None]
    base = dot(flat_edges, w_edge_one).reshape(row_count, nbr_count, edge_width)
    base = (base + src_proj[:, None, :].astype(f32)).reshape(-1, edge_width)
    grad_agg = dot(node_cot, w_node.T)
    grad_new = edge_cot.astype(f32) + masked * grad_agg[:, None, :] * agg_scale
    grad_upd = (masked * grad_new).astype(bf16).reshape(-1, edge_width)
    grad_up = dot(grad_upd, w_edge_three.T)

    table, base, grad_up, node_late = lax.optimization_barrier((table, base, grad_up, node_in))
    node_column = spread(node_late, (RING,)).reshape(-1, node_in.shape[1])
    act_one, act_two, grad_pre_two, grad_pre_one, partial = edge_chain(
        places, table, base, grad_up, w_edge_two
    )
    act_one, act_two, grad_pre_two, grad_pre_one, node_column, partial = lax.optimization_barrier(
        (act_one, act_two, grad_pre_two, grad_pre_one, node_column, partial)
    )
    arriving = exchange(partial.reshape(deep * wide, -1, edge_width), PLANE)

    update = dot(act_two, w_edge_three).reshape(row_count, nbr_count, edge_width)
    edge_new = edge_in.astype(f32) + masked * update
    edge_out = edge_new.astype(bf16)
    aggregate = (jnp.sum(masked * edge_new, axis=1) * agg_scale).astype(bf16)
    node_out = (node_in.astype(f32) + dot(aggregate, w_node)).astype(bf16)
    back_edge = dot(grad_pre_one, w_edge_one.T).reshape(row_count, nbr_count, edge_width)
    grad_edge = (grad_new + back_edge).astype(bf16)
    grad_src = jnp.sum(
        grad_pre_one.reshape(row_count, nbr_count, edge_width).astype(f32), axis=1
    ).astype(bf16)
    grad_node = node_cot.astype(f32) + dot(grad_src, w_src.T)

    term_node = dot(aggregate.T, node_cot)
    terms = [
        dot(node_in.T, grad_src),
        dot(flat_edges.T, grad_pre_one),
        dot(act_one.T, grad_pre_two),
        dot(act_two.T, grad_upd),
    ]
    terms += [term_node[:, at : at + edge_width] for at in range(0, term_node.shape[1], edge_width)]
    early = jnp.concatenate([term.astype(bf16) for term in terms], axis=0)
    done = (node_out, edge_out, grad_edge, grad_node, early, arriving)
    node_out, edge_out, grad_edge, grad_node, early, arriving = lax.optimization_barrier(done)

    partial = sum_first(arriving).astype(bf16)
    grad_dst = sum_first(exchange(partial.reshape(long, row_count, edge_width), (RING,)))
    grad_dst = grad_dst.astype(bf16)
    terms.append(dot(node_column.T, partial))
    starts = [0]
    for term in terms:
        starts.append(starts[-1] + term.shape[0])
    height = -(-starts[-1] // (parts * 16)) * 16
    blank = jnp.zeros((parts * height - starts[-1], edge_width), bf16)
    packed = jnp.concatenate([early, terms[-1].astype(bf16), blank], axis=0)
    own = sum_first(exchange(packed.reshape(parts, height, edge_width), ALL)).astype(bf16)
    sums = spread(own, ALL).reshape(-1, edge_width).astype(f32)
    sums = [sums[low:high] for low, high in zip(starts[:-1], starts[1:])]

    grad_node = (grad_node + dot(grad_dst, w_dst.T)).astype(bf16)
    return (
        node_out,
        edge_out,
        grad_node,
        grad_edge,
        sums[0] * node_scale,
        sums[-1] * node_scale,
        sums[1] * edge_scale,
        sums[2] * edge_scale,
        sums[3] * edge_scale,
        jnp.concatenate(sums[4:-1], axis=1) * node_scale,
    )


def solution(mesh):
    shape = mesh.shape
    outer = shape["node"]
    inner = outer
    devices = mesh.devices.reshape(shape["cplx"], outer, shape["edge"] // inner, inner)
    mesh = Mesh(devices, ("cplx", *ALL))
    in_specs = (
        P(("cplx", *ALL), None),
        P(("cplx", *ALL), None, None),
        P(("cplx", *ALL), None),
        P(("cplx", *ALL), None),
        P(),
        P(),
        P(),
        P(),
        P(),
        P(),
        P(("cplx", *ALL), None),
        P(("cplx", *ALL), None, None),
    )
    out_specs = (
        P(("cplx", *ALL), None),
        P(("cplx", *ALL), None, None),
        P(("cplx", *ALL), None),
        P(("cplx", *ALL), None, None),
        P("cplx", None),
        P("cplx", None),
        P("cplx", None),
        P("cplx", None),
        P("cplx", None),
        P("cplx", None),
    )
    return jax.shard_map(shards, mesh=mesh, in_specs=in_specs, out_specs=out_specs, check_vma=False)
```

```python
import functools
import math

import jax
import jax.numpy as jnp
from jax import lax
from jax.experimental import pallas as pl
from jax.experimental.pallas import tpu as pltpu
from jax.sharding import Mesh
from jax.sharding import PartitionSpec as P

RING = ("z",)
COLUMN = ("y", "z")
PLANE = ("x", "y")
ALL = ("y", "z", "x")
SUMS = 4
UNROLL = 32
BLOCK = 1024
CHUNK = 1024
PIECE = 512


def exchange(value, axes):
    return lax.all_to_all(value, axes, 0, 0, tiled=True)


def spread(value, axes):
    count = math.prod(lax.axis_size(axis) for axis in axes)
    return exchange(jnp.broadcast_to(value[None], (count, *value.shape)), axes)


def sum_first(value):
    return jnp.sum(value.astype(jnp.float32), axis=0)


def deriv(value, sigma_val):
    return sigma_val * (1.0 + value * (1.0 - sigma_val))

def sigmoid(v):
    return 0.5 * jnp.tanh(0.5 * v) + 0.5

def dot(left, right):
    return jnp.dot(left, right, preferred_element_type=jnp.float32)

def dot_turned(left, right):
    return lax.dot_general(left, right, (((1,), (1,)), ((), ())), preferred_element_type=jnp.float32)

def dot_rows(left, right):
    return lax.dot_general(left, right, (((0,), (0,)), ((), ())), preferred_element_type=jnp.float32)

def edge_layer_body(agg_scale,
    place_ref, table_ref, edge_ref, cot_ref, mask_ref, node_ref, node_cot_ref, w_src_ref, one_ref, two_ref, three_ref, w_node_ref,
    edge_out_ref, grad_edge_ref, message_ref, node_out_ref, grad_node_ref,
    table, pulled, grads, src_proj, grad_agg, aggregate, grad_src, early, *sums):
    step = pl.program_id(0)
    block = pulled.shape[0]
    count, width = table.shape
    nodes, deep = node_ref.shape
    nbrs = mask_ref.shape[1]
    groups = block // nbrs
    bf16, f32 = jnp.bfloat16, jnp.float32

    @pl.when(step == 0)
    def _():
        def fill(at, carry):
            rows = pl.ds(pl.multiple_of(at * PIECE, PIECE), PIECE)
            table[rows, :] = table_ref[rows, :].astype(f32)
            for one in sums:
                one[rows, :] = jnp.zeros((PIECE, width), f32)
            return carry
        lax.fori_loop(0, count // PIECE, fill, 0)
        early[...] = jnp.zeros(early.shape, f32)
        src_proj[...] = dot(node_ref[...], w_src_ref[...]).astype(bf16).astype(f32)
        grad_agg[...] = dot_turned(node_cot_ref[...], w_node_ref[...])

    first = step * block

    def pull(at, carry):
        low = at * UNROLL
        for k in range(UNROLL):
            pulled[pl.ds(low + k, 1), :] = table[pl.ds(place_ref[first + low + k], 1), :]
        return carry

    lax.fori_loop(0, block // UNROLL, pull, 0)

    row = pl.multiple_of(step * groups, groups)
    src_rows = src_proj[pl.ds(row, groups), :]
    agg_rows = grad_agg[pl.ds(row, groups), :]
    mask = mask_ref[...].astype(f32).T
    added, grouped = [], []
    per = CHUNK // nbrs
    for low in range(0, block, CHUNK):
        span = pl.ds(low, CHUNK)
        own = range(low // nbrs, low // nbrs + per)
        lay = lambda rows: jnp.concatenate([jnp.broadcast_to(rows[j : j + 1, :], (nbrs, width)) for j in own], axis=0)
        masked = jnp.concatenate([jnp.broadcast_to(mask[:, j : j + 1], (nbrs, width)) for j in own], axis=0)
        edges = edge_ref[span, :]
        grad_new = cot_ref[span, :].astype(f32) + masked * lay(agg_rows) * agg_scale
        grad_upd = (masked * grad_new).astype(bf16)
        pre_one = dot(edges, one_ref[...]) + lay(src_rows) + pulled[span, :]
        sigma_one = sigmoid(pre_one)
        act_one = (pre_one * sigma_one).astype(bf16)
        pre_two = dot(act_one, two_ref[...])
        sigma_two = sigmoid(pre_two)
        act_two = (pre_two * sigma_two).astype(bf16)
        edge_new = edges.astype(f32) + masked * dot(act_two, three_ref[...])
        edge_out_ref[span, :] = edge_new.astype(bf16)
        kept = masked * edge_new
        grad_two = (dot_turned(grad_upd, three_ref[...]) * deriv(pre_two, sigma_two)).astype(bf16)
        grad_one = (dot_turned(grad_two, two_ref[...]) * deriv(pre_one, sigma_one)).astype(bf16)
        grad_wide = grad_one.astype(f32)
        grads[span, :] = grad_wide
        grad_edge_ref[span, :] = (grad_new + dot_turned(grad_one, one_ref[...])).astype(bf16)
        for j in range(per):
            part = slice(j * nbrs, (j + 1) * nbrs)
            added.append(jnp.sum(kept[part], axis=0, keepdims=True))
            grouped.append(jnp.sum(grad_wide[part], axis=0, keepdims=True))
        for at, left, right in ((0, edges, grad_one), (1, act_one, grad_two), (2, act_two, grad_upd)):
            place = pl.ds(deep + at * width, width)
            early[place, :] += dot_rows(left, right)
    aggregate[pl.ds(row, groups), :] = jnp.concatenate(added, axis=0) * agg_scale
    grad_src[pl.ds(row, groups), :] = jnp.concatenate(grouped, axis=0)

    def push(at, carry):
        low = at * UNROLL
        for k in range(UNROLL):
            one = sums[k % len(sums)]
            place = pl.ds(place_ref[first + low + k], 1)
            one[place, :] += grads[pl.ds(low + k, 1), :]
        return carry

    lax.fori_loop(0, block // UNROLL, push, 0)

    @pl.when(step == pl.num_programs(0) - 1)
    def _():
        agg = aggregate[...].astype(bf16)
        node_out_ref[...] = (node_ref[...].astype(f32) + dot(agg, w_node_ref[...])).astype(bf16)
        src = grad_src[...].astype(bf16)
        grad_node_ref[...] = node_cot_ref[...].astype(f32) + dot_turned(src, w_src_ref[...])
        early[pl.ds(0, deep), :] = dot_rows(node_ref[...], src)
        for at in range(0, deep, width):
            early[pl.ds(deep + 3 * width + at, width), :] = dot_rows(agg, node_cot_ref[:, pl.ds(at, width)])
        blocks, height, _ = message_ref.shape
        share = count // blocks
        extra = height - share

        def merge(at, carry):
            rows = pl.ds(pl.multiple_of(at * share, share), share)
            value = sums[0][rows, :]
            for one in sums[1:]:
                value = value + one[rows, :]
            message_ref[at, pl.ds(0, share), :] = value.astype(bf16)
            rows = pl.ds(pl.multiple_of(at * extra, extra), extra)
            message_ref[at, pl.ds(share, extra), :] = early[rows, :].astype(bf16)
            return carry

        lax.fori_loop(0, blocks, merge, 0)


def edge_layer(places, table, edges, cots, mask, node_in, node_cot, w_src, w_one, w_two, w_three, w_node, blocks):
    count, width = table.shape
    total = places.shape[0]
    nodes, nbrs = mask.shape
    deep = node_in.shape[1]
    groups = BLOCK // nbrs
    extra = -(-(2 * deep + 3 * width) // (blocks * 16)) * 16
    f32, bf16 = jnp.float32, jnp.bfloat16
    rows = pl.BlockSpec((BLOCK, width), lambda i, places: (i, 0))
    def whole(*shape):
        return pl.BlockSpec(shape, lambda i, places: (0,) * len(shape))
    held = pltpu.VMEM((count, width), f32)
    part = pltpu.VMEM((BLOCK, width), f32)
    small = pltpu.VMEM((nodes, width), f32)
    return pl.pallas_call(
        functools.partial(edge_layer_body, 1.0 / math.sqrt(nbrs)),
        grid_spec=pltpu.PrefetchScalarGridSpec(
            num_scalar_prefetch=1,
            grid=(total // BLOCK,),
            in_specs=[whole(count, width), rows, rows, pl.BlockSpec((groups, nbrs), lambda i, places: (i, 0)),
              whole(nodes, deep), whole(nodes, deep), whole(deep, width), whole(width, width), whole(width, width), whole(width, width), whole(width, deep)],
            out_specs=[rows, rows, whole(blocks, count // blocks + extra, width), whole(nodes, deep), whole(nodes, deep)],
            scratch_shapes=[held, part, part, small, small, small, small, pltpu.VMEM((blocks * extra, width), f32)] + [held] * SUMS,
        ),
        out_shape=[jax.ShapeDtypeStruct((total, width), bf16)] * 2 + [jax.ShapeDtypeStruct((blocks, count // blocks + extra, width), bf16),
            jax.ShapeDtypeStruct((nodes, deep), bf16), jax.ShapeDtypeStruct((nodes, deep), f32)],
        compiler_params=pltpu.CompilerParams(vmem_limit_bytes=48 * 1024 * 1024),
        name="edge_layer",
    )(places, table, edges, cots, mask, node_in, node_cot, w_src, w_one, w_two, w_three, w_node)


def shards(
    node_in,
    edge_in,
    neighbours,
    edge_mask,
    w_src,
    w_dst,
    w_edge_one,
    w_edge_two,
    w_edge_three,
    w_node,
    node_cot,
    edge_cot,
):
    row_count, nbr_count, width = edge_in.shape
    deep = node_in.shape[1]
    bf16, f32 = jnp.bfloat16, jnp.float32
    long, tall, wide = lax.axis_size("z"), lax.axis_size("y"), lax.axis_size("x")
    blocks = wide * tall
    total = blocks * long * row_count
    node_scale = 1.0 / math.sqrt(total)
    edge_scale = 1.0 / math.sqrt(total * nbr_count)

    column = spread(dot(node_in, w_dst).astype(bf16), COLUMN)
    own_row, rest = neighbours % row_count, neighbours // row_count
    at_x, rest = rest % wide, rest // wide
    places = ((at_x * (tall * long) + rest) * row_count + own_row).reshape(-1)
    column, places, node_late = lax.optimization_barrier((column, places, jnp.concatenate([node_in, node_cot], axis=1)))
    table = spread(column.reshape(-1, width), ("x",)).reshape(total, width)
    node_column = lax.all_gather(node_late, "z", axis=0, tiled=True)

    edge_out, grad_edge, message, node_out, grad_node = edge_layer(
        places,
        table,
        edge_in.reshape(row_count * nbr_count, width),
        edge_cot.reshape(row_count * nbr_count, width),
        edge_mask,
        node_in,
        node_cot,
        w_src,
        w_edge_one,
        w_edge_two,
        w_edge_three,
        w_node,
        blocks,
    )
    share = long * row_count
    arriving = exchange(message, PLANE)
    partial = sum_first(arriving[:, :share]).astype(bf16)
    early = sum_first(arriving[:, share:]).astype(bf16)
    late = dot_rows(node_column[:, :deep], partial).astype(bf16)
    late = sum_first(exchange(late.reshape(blocks, -1, width), PLANE)).astype(bf16)
    extra, rest = early.shape[0], late.shape[0]
    weights = jnp.broadcast_to(jnp.concatenate([early, late])[None], (long, extra + rest, width))
    packed = jnp.concatenate([partial.reshape(long, row_count, width), weights], axis=1)
    own = sum_first(exchange(packed, RING)).astype(bf16)
    grad_node = (grad_node + dot_turned(own[:row_count], w_dst)).astype(bf16)
    sums = spread(own[row_count:], PLANE).astype(f32)
    early = sums[:, :extra].reshape(-1, width)
    late = sums[:, extra:].reshape(-1, width)
    ones = [early[at : at + width] * edge_scale for at in range(deep, deep + 3 * width, width)]
    slabs = [early[at : at + width] for at in range(deep + 3 * width, 2 * deep + 3 * width, width)]
    return (
        node_out,
        edge_out.reshape(edge_in.shape),
        grad_node,
        grad_edge.reshape(edge_in.shape),
        early[:deep] * node_scale,
        late * node_scale,
        *ones,
        jnp.concatenate(slabs, axis=1) * node_scale,
    )


def solution(mesh):
    shape = mesh.shape
    outer = shape["node"]
    inner = outer
    devices = mesh.devices.reshape(shape["cplx"], outer, shape["edge"] // inner, inner)
    mesh = Mesh(devices, ("cplx", *ALL))
    in_specs = (
        P(("cplx", *ALL), None),
        P(("cplx", *ALL), None, None),
        P(("cplx", *ALL), None),
        P(("cplx", *ALL), None),
        P(),
        P(),
        P(),
        P(),
        P(),
        P(),
        P(("cplx", *ALL), None),
        P(("cplx", *ALL), None, None),
    )
    out_specs = (
        P(("cplx", *ALL), None),
        P(("cplx", *ALL), None, None),
        P(("cplx", *ALL), None),
        P(("cplx", *ALL), None, None),
        P("cplx", None),
        P("cplx", None),
        P("cplx", None),
        P("cplx", None),
        P("cplx", None),
        P("cplx", None),
    )
    return jax.shard_map(shards, mesh=mesh, in_specs=in_specs, out_specs=out_specs, check_vma=False)
```

```python
import functools
import math

import jax
import jax.numpy as jnp
from jax import lax
from jax.experimental import pallas as pl
from jax.experimental.pallas import tpu as pltpu
from jax.sharding import Mesh
from jax.sharding import PartitionSpec as P

RING = ("z",)
COLUMN = ("y", "z")
PLANE = ("x", "y")
ALL = ("y", "z", "x")
SUMS = 4
UNROLL = 32
BLOCK = 1024
SIDE_BLOCK = 1024
PIECE = 512


def exchange(value, axes):
    return lax.all_to_all(value, axes, 0, 0, tiled=True)


def spread(value, axes):
    count = math.prod(lax.axis_size(axis) for axis in axes)
    return exchange(jnp.broadcast_to(value[None], (count, *value.shape)), axes)


def sum_first(value):
    return jnp.sum(value.astype(jnp.float32), axis=0)


def sigmoid(value):
    return 0.5 * jnp.tanh(0.5 * value) + 0.5


def deriv(value, sigma_val):
    return sigma_val * (1.0 + value * (1.0 - sigma_val))


def dot(left, right):
    return jnp.dot(left, right, preferred_element_type=jnp.float32)


def dot_turned(left, right):
    return lax.dot_general(
        left, right, (((1,), (1,)), ((), ())), preferred_element_type=jnp.float32
    )


def dot_rows(left, right):
    return lax.dot_general(
        left, right, (((0,), (0,)), ((), ())), preferred_element_type=jnp.float32
    )


def rows_of(values, count):
    width = values.shape[1]
    rows = [jnp.broadcast_to(values[j : j + 1, :], (count, width)) for j in range(values.shape[0])]
    return jnp.concatenate(rows, axis=0)


def mask_of(mask, width):
    turned = mask.astype(jnp.float32).T
    count = turned.shape[0]
    columns = [jnp.broadcast_to(turned[:, j : j + 1], (count, width)) for j in range(mask.shape[0])]
    return jnp.concatenate(columns, axis=0)


def chain_body(
    agg_scale,
    place_ref,
    table_ref,
    edge_ref,
    cot_ref,
    mask_ref,
    node_ref,
    node_cot_ref,
    w_src_ref,
    one_ref,
    two_ref,
    three_ref,
    w_node_ref,
    act_one_ref,
    act_two_ref,
    grad_two_ref,
    grad_one_ref,
    message_ref,
    table,
    pulled,
    grads,
    src_proj,
    grad_agg,
    *sums,
):
    step = pl.program_id(0)
    block = pulled.shape[0]
    count, width = table.shape
    groups, nbrs = mask_ref.shape
    bf16, f32 = jnp.bfloat16, jnp.float32

    @pl.when(step == 0)
    def _():
        def fill(at, carry):
            rows = pl.ds(pl.multiple_of(at * PIECE, PIECE), PIECE)
            table[rows, :] = table_ref[rows, :].astype(f32)
            for one in sums:
                one[rows, :] = jnp.zeros((PIECE, width), f32)
            return carry

        lax.fori_loop(0, count // PIECE, fill, 0)
        src_proj[...] = dot(node_ref[...], w_src_ref[...]).astype(bf16).astype(f32)
        grad_agg[...] = dot_turned(node_cot_ref[...], w_node_ref[...]) * agg_scale

    first = step * block

    def pull(at, carry):
        low = at * UNROLL
        for k in range(UNROLL):
            pulled[pl.ds(low + k, 1), :] = table[pl.ds(place_ref[first + low + k], 1), :]
        return carry

    lax.fori_loop(0, block // UNROLL, pull, 0)

    row = pl.multiple_of(step * groups, groups)
    masked = mask_of(mask_ref[...], width)
    agg_rows = rows_of(grad_agg[pl.ds(row, groups), :], nbrs)
    grad_upd = (masked * (cot_ref[...].astype(f32) + masked * agg_rows)).astype(bf16)
    pre_one = dot(edge_ref[...], one_ref[...]) + rows_of(src_proj[pl.ds(row, groups), :], nbrs)
    pre_one = pre_one + pulled[...]
    sigma_one = sigmoid(pre_one)
    act_one = (pre_one * sigma_one).astype(bf16)
    act_one_ref[...] = act_one
    pre_two = dot(act_one, two_ref[...])
    sigma_two = sigmoid(pre_two)
    act_two_ref[...] = (pre_two * sigma_two).astype(bf16)
    grad_two = (dot_turned(grad_upd, three_ref[...]) * deriv(pre_two, sigma_two)).astype(bf16)
    grad_two_ref[...] = grad_two
    grad_one = (dot_turned(grad_two, two_ref[...]) * deriv(pre_one, sigma_one)).astype(bf16)
    grad_one_ref[...] = grad_one
    grads[...] = grad_one.astype(f32)

    def push(at, carry):
        low = at * UNROLL
        for k in range(UNROLL):
            one = sums[k % len(sums)]
            place = pl.ds(place_ref[first + low + k], 1)
            one[place, :] += grads[pl.ds(low + k, 1), :]
        return carry

    lax.fori_loop(0, block // UNROLL, push, 0)

    @pl.when(step == pl.num_programs(0) - 1)
    def _():
        def merge(at, carry):
            rows = pl.ds(pl.multiple_of(at * PIECE, PIECE), PIECE)
            value = sums[0][rows, :]
            for one in sums[1:]:
                value = value + one[rows, :]
            message_ref[rows, :] = value.astype(bf16)
            return carry

        lax.fori_loop(0, count // PIECE, merge, 0)


def whole(*shape):
    return pl.BlockSpec(shape, lambda i, *places: (0,) * len(shape))


def edge_chain(
    places, table, edges, cots, mask, node_in, node_cot, w_src, w_one, w_two, w_three, w_node
):
    count, width = table.shape
    total = places.shape[0]
    nodes, nbrs = mask.shape
    deep = node_in.shape[1]
    f32, bf16 = jnp.float32, jnp.bfloat16
    rows = pl.BlockSpec((BLOCK, width), lambda i, places: (i, 0))
    masks = pl.BlockSpec((BLOCK // nbrs, nbrs), lambda i, places: (i, 0))
    square = whole(width, width)
    held = pltpu.VMEM((count, width), f32)
    part = pltpu.VMEM((BLOCK, width), f32)
    small = pltpu.VMEM((nodes, width), f32)
    return pl.pallas_call(
        functools.partial(chain_body, 1.0 / math.sqrt(nbrs)),
        grid_spec=pltpu.PrefetchScalarGridSpec(
            num_scalar_prefetch=1,
            grid=(total // BLOCK,),
            in_specs=[whole(count, width), rows, rows, masks, whole(nodes, deep)]
            + [whole(nodes, deep), whole(deep, width), square, square, square, whole(width, deep)],
            out_specs=[rows] * 4 + [whole(count, width)],
            scratch_shapes=[held, part, part, small, small] + [held] * SUMS,
        ),
        out_shape=[jax.ShapeDtypeStruct((total, width), bf16)] * 4
        + [jax.ShapeDtypeStruct((count, width), bf16)],
        compiler_params=pltpu.CompilerParams(vmem_limit_bytes=44 * 1024 * 1024),
        cost_estimate=pl.CostEstimate(
            flops=8 * total * width * width, bytes_accessed=12 * 2**20, transcendentals=0
        ),
        name="edge_chain",
    )(places, table, edges, cots, mask, node_in, node_cot, w_src, w_one, w_two, w_three, w_node)


def side_body(
    agg_scale,
    edge_ref,
    cot_ref,
    mask_ref,
    act_one_ref,
    act_two_ref,
    grad_two_ref,
    grad_one_ref,
    node_ref,
    node_cot_ref,
    w_src_ref,
    one_ref,
    three_ref,
    w_node_ref,
    edge_out_ref,
    grad_edge_ref,
    early_ref,
    node_out_ref,
    grad_node_ref,
    grad_agg,
    aggregate,
    grad_src,
    terms,
):
    step = pl.program_id(0)
    groups, nbrs = mask_ref.shape
    width = edge_ref.shape[1]
    deep = node_ref.shape[1]
    bf16, f32 = jnp.bfloat16, jnp.float32

    @pl.when(step == 0)
    def _():
        terms[...] = jnp.zeros(terms.shape, f32)
        grad_agg[...] = dot_turned(node_cot_ref[...], w_node_ref[...]) * agg_scale

    row = pl.multiple_of(step * groups, groups)
    masked = mask_of(mask_ref[...], width)
    grad_new = cot_ref[...].astype(f32) + masked * rows_of(grad_agg[pl.ds(row, groups), :], nbrs)
    grad_upd = (masked * grad_new).astype(bf16)
    grad_one = grad_one_ref[...]
    grad_edge_ref[...] = (grad_new + dot_turned(grad_one, one_ref[...])).astype(bf16)
    edges = edge_ref[...]
    act_two = act_two_ref[...]
    edge_new = edges.astype(f32) + masked * dot(act_two, three_ref[...])
    edge_out_ref[...] = edge_new.astype(bf16)
    kept = masked * edge_new
    grad_wide = grad_one.astype(f32)
    added, grouped = [], []
    for j in range(groups):
        part = slice(j * nbrs, (j + 1) * nbrs)
        added.append(jnp.sum(kept[part], axis=0, keepdims=True))
        grouped.append(jnp.sum(grad_wide[part], axis=0, keepdims=True))
    aggregate[pl.ds(row, groups), :] = jnp.concatenate(added, axis=0) * agg_scale
    grad_src[pl.ds(row, groups), :] = jnp.concatenate(grouped, axis=0)
    pairs = ((edges, grad_one), (act_one_ref[...], grad_two_ref[...]), (act_two, grad_upd))
    for at, (left, right) in enumerate(pairs):
        terms[pl.ds(at * width, width), :] += dot_rows(left, right)

    @pl.when(step == pl.num_programs(0) - 1)
    def _():
        agg = aggregate[...].astype(bf16)
        node_out_ref[...] = (node_ref[...].astype(f32) + dot(agg, w_node_ref[...])).astype(bf16)
        src = grad_src[...].astype(bf16)
        grad_node_ref[...] = node_cot_ref[...].astype(f32) + dot_turned(src, w_src_ref[...])
        early_ref[pl.ds(0, deep), :] = dot_rows(node_ref[...], src).astype(bf16)
        early_ref[pl.ds(deep, 3 * width), :] = terms[...].astype(bf16)
        low = deep + 3 * width
        for at in range(0, deep, width):
            slab = dot_rows(agg, node_cot_ref[:, pl.ds(at, width)])
            early_ref[pl.ds(low + at, width), :] = slab.astype(bf16)
        low = low + deep
        rest = early_ref.shape[0] - low
        early_ref[pl.ds(low, rest), :] = jnp.zeros((rest, width), bf16)


def edge_side(
    edges, cots, mask, chain, node_in, node_cot, w_src, w_one, w_three, w_node, early_rows
):
    total, width = edges.shape
    nodes, nbrs = mask.shape
    deep = node_in.shape[1]
    f32, bf16 = jnp.float32, jnp.bfloat16
    rows = pl.BlockSpec((SIDE_BLOCK, width), lambda i: (i, 0))
    masks = pl.BlockSpec((SIDE_BLOCK // nbrs, nbrs), lambda i: (i, 0))
    square = whole(width, width)
    small = pltpu.VMEM((nodes, width), f32)
    return pl.pallas_call(
        functools.partial(side_body, 1.0 / math.sqrt(nbrs)),
        grid=(total // SIDE_BLOCK,),
        in_specs=[rows, rows, masks] + [rows] * 4 + [whole(nodes, deep), whole(nodes, deep)]
        + [whole(deep, width), square, square, whole(width, deep)],
        out_specs=[rows, rows, whole(early_rows, width), whole(nodes, deep), whole(nodes, deep)],
        scratch_shapes=[small, small, small, pltpu.VMEM((3 * width, width), f32)],
        out_shape=[jax.ShapeDtypeStruct((total, width), bf16)] * 2
        + [jax.ShapeDtypeStruct((early_rows, width), bf16)]
        + [jax.ShapeDtypeStruct((nodes, deep), bf16), jax.ShapeDtypeStruct((nodes, deep), f32)],
        compiler_params=pltpu.CompilerParams(vmem_limit_bytes=24 * 1024 * 1024),
        cost_estimate=pl.CostEstimate(
            flops=10 * total * width * width, bytes_accessed=24 * 2**20, transcendentals=0
        ),
        name="edge_side",
    )(edges, cots, mask, *chain, node_in, node_cot, w_src, w_one, w_three, w_node)


def meet_body(arriving_ref, node_ref, early_ref, partial_ref, message_ref):
    blocks, share, width = arriving_ref.shape
    bf16, f32 = jnp.bfloat16, jnp.float32
    value = arriving_ref[0].astype(f32)
    for at in range(1, blocks):
        value = value + arriving_ref[at].astype(f32)
    partial = value.astype(bf16)
    partial_ref[...] = partial
    late = dot_rows(node_ref[...], partial).astype(bf16)
    rest = late.shape[0] // blocks
    extra = early_ref.shape[0] // blocks
    for at in range(blocks):
        message_ref[at, pl.ds(0, extra), :] = early_ref[pl.ds(at * extra, extra), :]
        message_ref[at, pl.ds(extra, rest), :] = late[at * rest : (at + 1) * rest]


def meet(arriving, node_column, early):
    blocks, share, width = arriving.shape
    deep = node_column.shape[1] // 2
    height = (early.shape[0] + deep) // blocks
    return pl.pallas_call(
        meet_body,
        grid=(1,),
        in_specs=[whole(*arriving.shape), whole(share, deep), whole(*early.shape)],
        out_specs=[whole(share, width), whole(blocks, height, width)],
        out_shape=[
            jax.ShapeDtypeStruct((share, width), jnp.bfloat16),
            jax.ShapeDtypeStruct((blocks, height, width), jnp.bfloat16),
        ],
        compiler_params=pltpu.CompilerParams(vmem_limit_bytes=24 * 1024 * 1024),
        cost_estimate=pl.CostEstimate(
            flops=2 * share * deep * width, bytes_accessed=4 * 2**20, transcendentals=0
        ),
        name="meet",
    )(arriving, node_column, early)


def shards(
    node_in,
    edge_in,
    neighbours,
    edge_mask,
    w_src,
    w_dst,
    w_edge_one,
    w_edge_two,
    w_edge_three,
    w_node,
    node_cot,
    edge_cot,
):
    row_count, nbr_count, width = edge_in.shape
    deep = node_in.shape[1]
    bf16, f32 = jnp.bfloat16, jnp.float32
    long, tall, wide = lax.axis_size("z"), lax.axis_size("y"), lax.axis_size("x")
    blocks = wide * tall
    total = blocks * long * row_count
    node_scale = 1.0 / math.sqrt(total)
    edge_scale = 1.0 / math.sqrt(total * nbr_count)

    column = spread(dot(node_in, w_dst).astype(bf16), COLUMN)
    own_row, rest = neighbours % row_count, neighbours // row_count
    at_x, rest = rest % wide, rest // wide
    places = ((at_x * (tall * long) + rest) * row_count + own_row).reshape(-1)
    column, places, node_late = lax.optimization_barrier((column, places, jnp.concatenate([node_in, node_cot], axis=1)))
    table = spread(column.reshape(-1, width), ("x",)).reshape(total, width)
    node_column = lax.all_gather(node_late, "z", axis=0, tiled=True)

    edges = edge_in.reshape(row_count * nbr_count, width)
    cots = edge_cot.reshape(row_count * nbr_count, width)
    *chain, message = edge_chain(
        places,
        table,
        edges,
        cots,
        edge_mask,
        node_in,
        node_cot,
        w_src,
        w_edge_one,
        w_edge_two,
        w_edge_three,
        w_node,
    )
    *chain, message, node_column = lax.optimization_barrier((*chain, message, node_column))
    arriving = exchange(message.reshape(blocks, -1, width), PLANE)
    extra = -(-(2 * deep + 3 * width) // (blocks * 16)) * 16
    edge_out, grad_edge, early, node_out, grad_node = edge_side(
        edges,
        cots,
        edge_mask,
        chain,
        node_in,
        node_cot,
        w_src,
        w_edge_one,
        w_edge_three,
        w_node,
        blocks * extra,
    )
    partial, message = meet(arriving, node_column, early)
    weights = sum_first(exchange(message, PLANE)).astype(bf16)
    weights = jnp.broadcast_to(weights[None], (long, *weights.shape))
    packed = jnp.concatenate([partial.reshape(long, row_count, width), weights], axis=1)
    own = sum_first(exchange(packed, RING)).astype(bf16)
    grad_node = (grad_node + dot_turned(own[:row_count], w_dst)).astype(bf16)
    sums = spread(own[row_count:], PLANE).astype(f32)
    early = sums[:, :extra].reshape(-1, width)
    late = sums[:, extra:].reshape(-1, width)
    ones = [early[at : at + width] * edge_scale for at in range(deep, deep + 3 * width, width)]
    slabs = [early[at : at + width] for at in range(deep + 3 * width, 2 * deep + 3 * width, width)]
    return (
        node_out,
        edge_out.reshape(edge_in.shape),
        grad_node,
        grad_edge.reshape(edge_in.shape),
        early[:deep] * node_scale,
        late * node_scale,
        *ones,
        jnp.concatenate(slabs, axis=1) * node_scale,
    )


def solution(mesh):
    shape = mesh.shape
    outer = shape["node"]
    inner = outer
    devices = mesh.devices.reshape(shape["cplx"], outer, shape["edge"] // inner, inner)
    mesh = Mesh(devices, ("cplx", *ALL))
    in_specs = (
        P(("cplx", *ALL), None),
        P(("cplx", *ALL), None, None),
        P(("cplx", *ALL), None),
        P(("cplx", *ALL), None),
        P(),
        P(),
        P(),
        P(),
        P(),
        P(),
        P(("cplx", *ALL), None),
        P(("cplx", *ALL), None, None),
    )
    out_specs = (
        P(("cplx", *ALL), None),
        P(("cplx", *ALL), None, None),
        P(("cplx", *ALL), None),
        P(("cplx", *ALL), None, None),
        P("cplx", None),
        P("cplx", None),
        P("cplx", None),
        P("cplx", None),
        P("cplx", None),
        P("cplx", None),
    )
    return jax.shard_map(shards, mesh=mesh, in_specs=in_specs, out_specs=out_specs, check_vma=False)
```

```python
import functools
import math

import jax
import jax.numpy as jnp
from jax import lax
from jax.experimental import pallas as pl
from jax.experimental.pallas import tpu as pltpu
from jax.sharding import Mesh
from jax.sharding import PartitionSpec as P

RING = ("z",)
PLANE = ("x", "y")
ALL = ("y", "z", "x")
SUMS = 4
UNROLL = 32
BLOCK = 1024
SIDE_BLOCK = 1024
PIECE = 512


def exchange(value, axes):
    return lax.all_to_all(value, axes, 0, 0, tiled=True)


def spread(value, axes):
    count = math.prod(lax.axis_size(axis) for axis in axes)
    return exchange(jnp.broadcast_to(value[None], (count, *value.shape)), axes)


def sum_first(value):
    return jnp.sum(value.astype(jnp.float32), axis=0)


def sigmoid(value):
    return 0.5 * jnp.tanh(0.5 * value) + 0.5


def deriv(value, sigma_val):
    return sigma_val * (1.0 + value * (1.0 - sigma_val))


def dot(left, right):
    return jnp.dot(left, right, preferred_element_type=jnp.float32)


def dot_turned(left, right):
    return lax.dot_general(
        left, right, (((1,), (1,)), ((), ())), preferred_element_type=jnp.float32
    )


def dot_rows(left, right):
    return lax.dot_general(
        left, right, (((0,), (0,)), ((), ())), preferred_element_type=jnp.float32
    )


def rows_of(values, count):
    width = values.shape[1]
    rows = [jnp.broadcast_to(values[j : j + 1, :], (count, width)) for j in range(values.shape[0])]
    return jnp.concatenate(rows, axis=0)


def mask_of(mask, width):
    turned = mask.astype(jnp.float32).T
    count = turned.shape[0]
    columns = [jnp.broadcast_to(turned[:, j : j + 1], (count, width)) for j in range(mask.shape[0])]
    return jnp.concatenate(columns, axis=0)


def chain_body(
    agg_scale,
    place_ref,
    table_ref,
    edge_ref,
    cot_ref,
    mask_ref,
    node_ref,
    node_cot_ref,
    w_src_ref,
    one_ref,
    two_ref,
    three_ref,
    w_node_ref,
    act_one_ref,
    act_two_ref,
    grad_two_ref,
    grad_one_ref,
    message_ref,
    table,
    pulled,
    grads,
    src_proj,
    grad_agg,
    *sums,
):
    step = pl.program_id(0)
    block = pulled.shape[0]
    count, width = table.shape
    groups, nbrs = mask_ref.shape
    bf16, f32 = jnp.bfloat16, jnp.float32

    @pl.when(step == 0)
    def _():
        def fill(at, carry):
            rows = pl.ds(pl.multiple_of(at * PIECE, PIECE), PIECE)
            table[rows, :] = table_ref[rows, :].astype(f32)
            for one in sums:
                one[rows, :] = jnp.zeros((PIECE, width), f32)
            return carry

        lax.fori_loop(0, count // PIECE, fill, 0)
        src_proj[...] = dot(node_ref[...], w_src_ref[...]).astype(bf16).astype(f32)
        grad_agg[...] = dot_turned(node_cot_ref[...], w_node_ref[...]) * agg_scale

    first = step * block

    def pull(at, carry):
        low = at * UNROLL
        for k in range(UNROLL):
            pulled[pl.ds(low + k, 1), :] = table[pl.ds(place_ref[first + low + k], 1), :]
        return carry

    lax.fori_loop(0, block // UNROLL, pull, 0)

    row = pl.multiple_of(step * groups, groups)
    masked = mask_of(mask_ref[...], width)
    agg_rows = rows_of(grad_agg[pl.ds(row, groups), :], nbrs)
    grad_upd = (masked * (cot_ref[...].astype(f32) + masked * agg_rows)).astype(bf16)
    pre_one = dot(edge_ref[...], one_ref[...]) + rows_of(src_proj[pl.ds(row, groups), :], nbrs)
    pre_one = pre_one + pulled[...]
    sigma_one = sigmoid(pre_one)
    act_one = (pre_one * sigma_one).astype(bf16)
    act_one_ref[...] = act_one
    pre_two = dot(act_one, two_ref[...])
    sigma_two = sigmoid(pre_two)
    act_two_ref[...] = (pre_two * sigma_two).astype(bf16)
    grad_two = (dot_turned(grad_upd, three_ref[...]) * deriv(pre_two, sigma_two)).astype(bf16)
    grad_two_ref[...] = grad_two
    grad_one = (dot_turned(grad_two, two_ref[...]) * deriv(pre_one, sigma_one)).astype(bf16)
    grad_one_ref[...] = grad_one
    grads[...] = grad_one.astype(f32)

    def push(at, carry):
        low = at * UNROLL
        for k in range(UNROLL):
            one = sums[k % len(sums)]
            place = pl.ds(place_ref[first + low + k], 1)
            one[place, :] += grads[pl.ds(low + k, 1), :]
        return carry

    lax.fori_loop(0, block // UNROLL, push, 0)

    @pl.when(step == pl.num_programs(0) - 1)
    def _():
        def merge(at, carry):
            rows = pl.ds(pl.multiple_of(at * PIECE, PIECE), PIECE)
            value = sums[0][rows, :]
            for one in sums[1:]:
                value = value + one[rows, :]
            message_ref[rows, :] = value.astype(bf16)
            return carry

        lax.fori_loop(0, count // PIECE, merge, 0)


def whole(*shape):
    return pl.BlockSpec(shape, lambda i, *places: (0,) * len(shape))


def in_hbm(value):
    return pltpu.with_memory_space_constraint(value, pltpu.HBM)


def edge_chain(
    places, table, edges, cots, mask, node_in, node_cot, w_src, w_one, w_two, w_three, w_node
):
    count, width = table.shape
    total = places.shape[0]
    nodes, nbrs = mask.shape
    deep = node_in.shape[1]
    f32, bf16 = jnp.float32, jnp.bfloat16
    rest = (cots, mask, node_in, node_cot, w_src, w_one, w_two, w_three, w_node)
    rest = tuple(map(in_hbm, rest))
    rows = pl.BlockSpec((BLOCK, width), lambda i, places: (i, 0))
    masks = pl.BlockSpec((BLOCK // nbrs, nbrs), lambda i, places: (i, 0))
    square = whole(width, width)
    held = pltpu.VMEM((count, width), f32)
    part = pltpu.VMEM((BLOCK, width), f32)
    small = pltpu.VMEM((nodes, width), f32)
    return pl.pallas_call(
        functools.partial(chain_body, 1.0 / math.sqrt(nbrs)),
        grid_spec=pltpu.PrefetchScalarGridSpec(
            num_scalar_prefetch=1,
            grid=(total // BLOCK,),
            in_specs=[whole(count, width), rows, rows, masks, whole(nodes, deep)]
            + [whole(nodes, deep), whole(deep, width), square, square, square, whole(width, deep)],
            out_specs=[rows] * 4 + [whole(count, width)],
            scratch_shapes=[held, part, part, small, small] + [held] * SUMS,
        ),
        out_shape=[pltpu.HBM((total, width), bf16)] * 4 + [pltpu.HBM((count, width), bf16)],
        compiler_params=pltpu.CompilerParams(vmem_limit_bytes=44 * 1024 * 1024),
        cost_estimate=pl.CostEstimate(
            flops=8 * total * width * width, bytes_accessed=12 * 2**20, transcendentals=0
        ),
        name="edge_chain",
    )(places, table, edges, *rest)


def side_body(
    agg_scale,
    edge_ref,
    cot_ref,
    mask_ref,
    act_one_ref,
    act_two_ref,
    grad_two_ref,
    grad_one_ref,
    node_ref,
    node_cot_ref,
    w_src_ref,
    one_ref,
    three_ref,
    w_node_ref,
    edge_out_ref,
    grad_edge_ref,
    early_ref,
    node_out_ref,
    grad_node_ref,
    grad_agg,
    aggregate,
    grad_src,
    terms,
):
    step = pl.program_id(0)
    groups, nbrs = mask_ref.shape
    width = edge_ref.shape[1]
    deep = node_ref.shape[1]
    bf16, f32 = jnp.bfloat16, jnp.float32

    @pl.when(step == 0)
    def _():
        terms[...] = jnp.zeros(terms.shape, f32)
        grad_agg[...] = dot_turned(node_cot_ref[...], w_node_ref[...]) * agg_scale

    row = pl.multiple_of(step * groups, groups)
    masked = mask_of(mask_ref[...], width)
    grad_new = cot_ref[...].astype(f32) + masked * rows_of(grad_agg[pl.ds(row, groups), :], nbrs)
    grad_upd = (masked * grad_new).astype(bf16)
    grad_one = grad_one_ref[...]
    grad_edge_ref[...] = (grad_new + dot_turned(grad_one, one_ref[...])).astype(bf16)
    edges = edge_ref[...]
    act_two = act_two_ref[...]
    edge_new = edges.astype(f32) + masked * dot(act_two, three_ref[...])
    edge_out_ref[...] = edge_new.astype(bf16)
    kept = masked * edge_new
    grad_wide = grad_one.astype(f32)
    added, grouped = [], []
    for j in range(groups):
        part = slice(j * nbrs, (j + 1) * nbrs)
        added.append(jnp.sum(kept[part], axis=0, keepdims=True))
        grouped.append(jnp.sum(grad_wide[part], axis=0, keepdims=True))
    aggregate[pl.ds(row, groups), :] = jnp.concatenate(added, axis=0) * agg_scale
    grad_src[pl.ds(row, groups), :] = jnp.concatenate(grouped, axis=0)
    pairs = ((edges, grad_one), (act_one_ref[...], grad_two_ref[...]), (act_two, grad_upd))
    for at, (left, right) in enumerate(pairs):
        terms[pl.ds(at * width, width), :] += dot_rows(left, right)

    @pl.when(step == pl.num_programs(0) - 1)
    def _():
        agg = aggregate[...].astype(bf16)
        node_out_ref[...] = (node_ref[...].astype(f32) + dot(agg, w_node_ref[...])).astype(bf16)
        src = grad_src[...].astype(bf16)
        grad_node_ref[...] = node_cot_ref[...].astype(f32) + dot_turned(src, w_src_ref[...])
        early_ref[pl.ds(0, deep), :] = dot_rows(node_ref[...], src).astype(bf16)
        early_ref[pl.ds(deep, 3 * width), :] = terms[...].astype(bf16)
        low = deep + 3 * width
        for at in range(0, deep, width):
            slab = dot_rows(agg, node_cot_ref[:, pl.ds(at, width)])
            early_ref[pl.ds(low + at, width), :] = slab.astype(bf16)
        low = low + deep
        rest = early_ref.shape[0] - low
        early_ref[pl.ds(low, rest), :] = jnp.zeros((rest, width), bf16)


def edge_side(
    edges, cots, mask, chain, node_in, node_cot, w_src, w_one, w_three, w_node, early_rows
):
    total, width = edges.shape
    nodes, nbrs = mask.shape
    rest = tuple(map(in_hbm, (node_in, node_cot, w_src, w_one, w_three, w_node)))
    deep = node_in.shape[1]
    f32, bf16 = jnp.float32, jnp.bfloat16
    rows = pl.BlockSpec((SIDE_BLOCK, width), lambda i: (i, 0))
    masks = pl.BlockSpec((SIDE_BLOCK // nbrs, nbrs), lambda i: (i, 0))
    square = whole(width, width)
    small = pltpu.VMEM((nodes, width), f32)
    return pl.pallas_call(
        functools.partial(side_body, 1.0 / math.sqrt(nbrs)),
        grid=(total // SIDE_BLOCK,),
        in_specs=[rows, rows, masks] + [rows] * 4 + [whole(nodes, deep), whole(nodes, deep)]
        + [whole(deep, width), square, square, whole(width, deep)],
        out_specs=[rows, rows, whole(early_rows, width), whole(nodes, deep), whole(nodes, deep)],
        scratch_shapes=[small, small, small, pltpu.VMEM((3 * width, width), f32)],
        out_shape=[pltpu.HBM((total, width), bf16)] * 2
        + [pltpu.HBM((early_rows, width), bf16)]
        + [pltpu.HBM((nodes, deep), bf16), pltpu.HBM((nodes, deep), f32)],
        compiler_params=pltpu.CompilerParams(vmem_limit_bytes=24 * 1024 * 1024),
        cost_estimate=pl.CostEstimate(
            flops=10 * total * width * width, bytes_accessed=24 * 2**20, transcendentals=0
        ),
        name="edge_side",
    )(*map(in_hbm, (edges, cots)), in_hbm(mask), *map(in_hbm, chain), *rest)


def meet_body(arriving_ref, node_ref, early_ref, partial_ref, message_ref):
    blocks, share, width = arriving_ref.shape
    bf16, f32 = jnp.bfloat16, jnp.float32
    value = arriving_ref[0].astype(f32)
    for at in range(1, blocks):
        value = value + arriving_ref[at].astype(f32)
    partial = value.astype(bf16)
    partial_ref[...] = partial
    late = dot_rows(node_ref[...], partial).astype(bf16)
    rest = late.shape[0] // blocks
    extra = early_ref.shape[0] // blocks
    for at in range(blocks):
        message_ref[at, pl.ds(0, extra), :] = early_ref[pl.ds(at * extra, extra), :]
        message_ref[at, pl.ds(extra, rest), :] = late[at * rest : (at + 1) * rest]


def meet(arriving, node_column, early):
    blocks, share, width = arriving.shape
    deep = node_column.shape[1] // 2
    height = (early.shape[0] + deep) // blocks
    return pl.pallas_call(
        meet_body,
        grid=(1,),
        in_specs=[whole(*arriving.shape), whole(share, deep), whole(*early.shape)],
        out_specs=[whole(share, width), whole(blocks, height, width)],
        out_shape=[
            jax.ShapeDtypeStruct((share, width), jnp.bfloat16),
            jax.ShapeDtypeStruct((blocks, height, width), jnp.bfloat16),
        ],
        compiler_params=pltpu.CompilerParams(vmem_limit_bytes=24 * 1024 * 1024),
        cost_estimate=pl.CostEstimate(
            flops=2 * share * deep * width, bytes_accessed=4 * 2**20, transcendentals=0
        ),
        name="meet",
    )(arriving, in_hbm(node_column), in_hbm(early))


def shards(
    node_in,
    edge_in,
    neighbours,
    edge_mask,
    w_src,
    w_dst,
    w_edge_one,
    w_edge_two,
    w_edge_three,
    w_node,
    node_cot,
    edge_cot,
):
    row_count, nbr_count, width = edge_in.shape
    deep = node_in.shape[1]
    bf16, f32 = jnp.bfloat16, jnp.float32
    long, tall, wide = lax.axis_size("z"), lax.axis_size("y"), lax.axis_size("x")
    blocks = wide * tall
    total = blocks * long * row_count
    node_scale = 1.0 / math.sqrt(total)
    edge_scale = 1.0 / math.sqrt(total * nbr_count)

    column = spread(dot(node_in, w_dst).astype(bf16), RING)
    own_row, rest = neighbours % row_count, neighbours // row_count
    at_x, rest = rest % wide, rest // wide
    places = ((at_x * (tall * long) + rest) * row_count + own_row).reshape(-1)
    column, places, node_late = lax.optimization_barrier((column, places, jnp.concatenate([node_in, node_cot], axis=1)))
    table = spread(column.reshape(-1, width), PLANE).reshape(total, width)
    node_column = lax.all_gather(node_late, "z", axis=0, tiled=True)

    edges = edge_in.reshape(row_count * nbr_count, width)
    cots = edge_cot.reshape(row_count * nbr_count, width)
    *chain, message = edge_chain(
        places,
        table,
        edges,
        cots,
        edge_mask,
        node_in,
        node_cot,
        w_src,
        w_edge_one,
        w_edge_two,
        w_edge_three,
        w_node,
    )
    *chain, message, node_column = lax.optimization_barrier((*chain, message, node_column))
    arriving = exchange(message.reshape(blocks, -1, width), PLANE)
    extra = -(-(2 * deep + 3 * width) // (blocks * 16)) * 16
    edge_out, grad_edge, early, node_out, grad_node = edge_side(
        edges,
        cots,
        edge_mask,
        chain,
        node_in,
        node_cot,
        w_src,
        w_edge_one,
        w_edge_three,
        w_node,
        blocks * extra,
    )
    partial, message = meet(arriving, node_column, early)
    weights = sum_first(exchange(message, PLANE)).astype(bf16)
    weights = jnp.broadcast_to(weights[None], (long, *weights.shape))
    packed = jnp.concatenate([partial.reshape(long, row_count, width), weights], axis=1)
    own = sum_first(exchange(packed, RING)).astype(bf16)
    grad_node = (grad_node + dot_turned(own[:row_count], w_dst)).astype(bf16)
    sums = spread(own[row_count:], PLANE).astype(f32)
    early = sums[:, :extra].reshape(-1, width)
    late = sums[:, extra:].reshape(-1, width)
    ones = [early[at : at + width] * edge_scale for at in range(deep, deep + 3 * width, width)]
    slabs = [early[at : at + width] for at in range(deep + 3 * width, 2 * deep + 3 * width, width)]
    return (
        node_out,
        edge_out.reshape(edge_in.shape),
        grad_node,
        grad_edge.reshape(edge_in.shape),
        early[:deep] * node_scale,
        late * node_scale,
        *ones,
        jnp.concatenate(slabs, axis=1) * node_scale,
    )


def solution(mesh):
    shape = mesh.shape
    outer = shape["node"]
    inner = outer
    devices = mesh.devices.reshape(shape["cplx"], outer, shape["edge"] // inner, inner)
    mesh = Mesh(devices, ("cplx", *ALL))
    in_specs = (
        P(("cplx", *ALL), None),
        P(("cplx", *ALL), None, None),
        P(("cplx", *ALL), None),
        P(("cplx", *ALL), None),
        P(),
        P(),
        P(),
        P(),
        P(),
        P(),
        P(("cplx", *ALL), None),
        P(("cplx", *ALL), None, None),
    )
    out_specs = (
        P(("cplx", *ALL), None),
        P(("cplx", *ALL), None, None),
        P(("cplx", *ALL), None),
        P(("cplx", *ALL), None, None),
        P("cplx", None),
        P("cplx", None),
        P("cplx", None),
        P("cplx", None),
        P("cplx", None),
        P("cplx", None),
    )
    return jax.shard_map(shards, mesh=mesh, in_specs=in_specs, out_specs=out_specs, check_vma=False)
```

```python
import functools
import math

import jax
import jax.numpy as jnp
from jax import lax
from jax.experimental import pallas as pl
from jax.experimental.pallas import tpu as pltpu
from jax.sharding import Mesh
from jax.sharding import PartitionSpec as P

RING = ("z",)
PLANE = ("x", "y")
ALL = ("y", "z", "x")
SUMS = 4
BLOCK = 1024
CHUNKS = 4
SIDE_BLOCK = 1024
PIECE = 512


def exchange(value, axes):
    return lax.all_to_all(value, axes, 0, 0, tiled=True)


def spread(value, axes):
    count = math.prod(lax.axis_size(axis) for axis in axes)
    return exchange(jnp.broadcast_to(value[None], (count, *value.shape)), axes)


def sum_first(value):
    return jnp.sum(value.astype(jnp.float32), axis=0)


def sigmoid(value):
    return 0.5 * jnp.tanh(0.5 * value) + 0.5


def deriv(value, sigma_val):
    return sigma_val * (1.0 + value * (1.0 - sigma_val))


def dot(left, right):
    return jnp.dot(left, right, preferred_element_type=jnp.float32)


def dot_turned(left, right):
    return lax.dot_general(
        left, right, (((1,), (1,)), ((), ())), preferred_element_type=jnp.float32
    )


def dot_rows(left, right):
    return lax.dot_general(
        left, right, (((0,), (0,)), ((), ())), preferred_element_type=jnp.float32
    )


def rows_of(values, count):
    width = values.shape[1]
    rows = [jnp.broadcast_to(values[j : j + 1, :], (count, width)) for j in range(values.shape[0])]
    return jnp.concatenate(rows, axis=0)


def mask_of(mask, width):
    turned = mask.astype(jnp.float32).T
    count = turned.shape[0]
    columns = [jnp.broadcast_to(turned[:, j : j + 1], (count, width)) for j in range(mask.shape[0])]
    return jnp.concatenate(columns, axis=0)


def prep_body(
    agg_scale,
    edge_ref,
    cot_ref,
    mask_ref,
    node_ref,
    node_cot_ref,
    w_src_ref,
    one_ref,
    three_ref,
    w_node_ref,
    base_ref,
    up_ref,
    src_proj,
    grad_agg,
):
    step = pl.program_id(0)
    groups, nbrs = mask_ref.shape
    width = edge_ref.shape[1]
    bf16, f32 = jnp.bfloat16, jnp.float32

    @pl.when(step == 0)
    def _():
        src_proj[...] = dot(node_ref[...], w_src_ref[...]).astype(bf16).astype(f32)
        grad_agg[...] = dot_turned(node_cot_ref[...], w_node_ref[...]) * agg_scale

    row = pl.multiple_of(step * groups, groups)
    masked = mask_of(mask_ref[...], width)
    agg_rows = rows_of(grad_agg[pl.ds(row, groups), :], nbrs)
    grad_upd = (masked * (cot_ref[...].astype(f32) + masked * agg_rows)).astype(bf16)
    up_ref[...] = dot_turned(grad_upd, three_ref[...])
    src_rows = rows_of(src_proj[pl.ds(row, groups), :], nbrs)
    base_ref[...] = dot(edge_ref[...], one_ref[...]) + src_rows


def in_hbm(value):
    return pltpu.with_memory_space_constraint(value, pltpu.HBM)


def whole(*shape):
    return pl.BlockSpec(shape, lambda i, *places: (0,) * len(shape))


def edge_prep(edges, cots, mask, node_in, node_cot, w_src, w_one, w_three, w_node):
    total, width = edges.shape
    nodes, nbrs = mask.shape
    deep = node_in.shape[1]
    rest = (edges, cots, mask, node_in, node_cot, w_src, w_one, w_three, w_node)
    rows = pl.BlockSpec((SIDE_BLOCK, width), lambda i: (i, 0))
    masks = pl.BlockSpec((SIDE_BLOCK // nbrs, nbrs), lambda i: (i, 0))
    square = whole(width, width)
    small = pltpu.VMEM((nodes, width), jnp.float32)
    return pl.pallas_call(
        functools.partial(prep_body, 1.0 / math.sqrt(nbrs)),
        grid=(total // SIDE_BLOCK,),
        in_specs=[rows, rows, masks, whole(nodes, deep), whole(nodes, deep), whole(deep, width)]
        + [square, square, whole(width, deep)],
        out_specs=[rows, rows],
        scratch_shapes=[small, small],
        out_shape=[pltpu.HBM((total, width), jnp.float32)] * 2,
        compiler_params=pltpu.CompilerParams(vmem_limit_bytes=24 * 1024 * 1024),
        cost_estimate=pl.CostEstimate(
            flops=4 * total * width * width, bytes_accessed=12 * 2**20, transcendentals=0
        ),
        name="edge_prep",
    )(*map(in_hbm, rest))


def chain_body(
    place_ref,
    table_ref,
    base_ref,
    up_ref,
    two_ref,
    act_one_ref,
    act_two_ref,
    grad_two_ref,
    grad_one_ref,
    message_ref,
    table,
    *held,
):
    step = pl.program_id(0)
    count, width = table.shape
    block = base_ref.shape[0]
    chunk = block // CHUNKS
    sums, pulled, grads = held[:SUMS], held[SUMS : SUMS + CHUNKS], held[SUMS + CHUNKS :]
    bf16, f32 = jnp.bfloat16, jnp.float32

    @pl.when(step == 0)
    def _():
        def fill(at, carry):
            rows = pl.ds(pl.multiple_of(at * PIECE, PIECE), PIECE)
            table[rows, :] = table_ref[rows, :].astype(f32)
            for one in sums:
                one[rows, :] = jnp.zeros((PIECE, width), f32)
            return carry

        lax.fori_loop(0, count // PIECE, fill, 0)

    first = step * block

    def pull(at):
        for k in range(chunk):
            place = place_ref[first + at * chunk + k]
            pulled[at][pl.ds(k, 1), :] = table[pl.ds(place, 1), :]

    def push(at):
        for k in range(chunk):
            one = sums[k % SUMS]
            place = pl.ds(place_ref[first + at * chunk + k], 1)
            one[place, :] += grads[at][pl.ds(k, 1), :]

    def work(at):
        span = pl.ds(at * chunk, chunk)
        pre_one = base_ref[span, :] + pulled[at][...]
        sigma_one = sigmoid(pre_one)
        act_one = (pre_one * sigma_one).astype(bf16)
        act_one_ref[span, :] = act_one
        pre_two = dot(act_one, two_ref[...])
        sigma_two = sigmoid(pre_two)
        act_two_ref[span, :] = (pre_two * sigma_two).astype(bf16)
        grad_two = (up_ref[span, :] * deriv(pre_two, sigma_two)).astype(bf16)
        grad_two_ref[span, :] = grad_two
        grad_one = (dot_turned(grad_two, two_ref[...]) * deriv(pre_one, sigma_one)).astype(bf16)
        grad_one_ref[span, :] = grad_one
        grads[at][...] = grad_one.astype(f32)

    pull(0)
    for at in range(CHUNKS):
        if at + 1 < CHUNKS:
            pull(at + 1)
        work(at)
        if at > 0:
            push(at - 1)
    push(CHUNKS - 1)

    @pl.when(step == pl.num_programs(0) - 1)
    def _():
        def merge(at, carry):
            rows = pl.ds(pl.multiple_of(at * PIECE, PIECE), PIECE)
            value = sums[0][rows, :]
            for one in sums[1:]:
                value = value + one[rows, :]
            message_ref[rows, :] = value.astype(bf16)
            return carry

        lax.fori_loop(0, count // PIECE, merge, 0)


def edge_chain(places, table, base, up, w_two):
    count, width = table.shape
    total = places.shape[0]
    f32, bf16 = jnp.float32, jnp.bfloat16
    rows = pl.BlockSpec((BLOCK, width), lambda i, places: (i, 0))
    held = pltpu.VMEM((count, width), f32)
    part = pltpu.VMEM((BLOCK // CHUNKS, width), f32)
    return pl.pallas_call(
        chain_body,
        grid_spec=pltpu.PrefetchScalarGridSpec(
            num_scalar_prefetch=1,
            grid=(total // BLOCK,),
            in_specs=[whole(count, width), rows, rows, whole(width, width)],
            out_specs=[rows] * 4 + [whole(count, width)],
            scratch_shapes=[held] + [held] * SUMS + [part] * (2 * CHUNKS),
        ),
        out_shape=[pltpu.HBM((total, width), bf16)] * 4 + [pltpu.HBM((count, width), bf16)],
        compiler_params=pltpu.CompilerParams(vmem_limit_bytes=44 * 1024 * 1024),
        cost_estimate=pl.CostEstimate(
            flops=8 * total * width * width, bytes_accessed=12 * 2**20, transcendentals=0
        ),
        name="edge_chain",
    )(places, table, in_hbm(base), in_hbm(up), in_hbm(w_two))


def side_body(
    agg_scale,
    edge_ref,
    cot_ref,
    mask_ref,
    act_one_ref,
    act_two_ref,
    grad_two_ref,
    grad_one_ref,
    node_ref,
    node_cot_ref,
    w_src_ref,
    one_ref,
    three_ref,
    w_node_ref,
    edge_out_ref,
    grad_edge_ref,
    early_ref,
    node_out_ref,
    grad_node_ref,
    grad_agg,
    aggregate,
    grad_src,
    terms,
):
    step = pl.program_id(0)
    groups, nbrs = mask_ref.shape
    width = edge_ref.shape[1]
    deep = node_ref.shape[1]
    bf16, f32 = jnp.bfloat16, jnp.float32

    @pl.when(step == 0)
    def _():
        terms[...] = jnp.zeros(terms.shape, f32)
        grad_agg[...] = dot_turned(node_cot_ref[...], w_node_ref[...]) * agg_scale

    row = pl.multiple_of(step * groups, groups)
    masked = mask_of(mask_ref[...], width)
    grad_new = cot_ref[...].astype(f32) + masked * rows_of(grad_agg[pl.ds(row, groups), :], nbrs)
    grad_upd = (masked * grad_new).astype(bf16)
    grad_one = grad_one_ref[...]
    grad_edge_ref[...] = (grad_new + dot_turned(grad_one, one_ref[...])).astype(bf16)
    edges = edge_ref[...]
    act_two = act_two_ref[...]
    edge_new = edges.astype(f32) + masked * dot(act_two, three_ref[...])
    edge_out_ref[...] = edge_new.astype(bf16)
    kept = masked * edge_new
    grad_wide = grad_one.astype(f32)
    added, grouped = [], []
    for j in range(groups):
        part = slice(j * nbrs, (j + 1) * nbrs)
        added.append(jnp.sum(kept[part], axis=0, keepdims=True))
        grouped.append(jnp.sum(grad_wide[part], axis=0, keepdims=True))
    aggregate[pl.ds(row, groups), :] = jnp.concatenate(added, axis=0) * agg_scale
    grad_src[pl.ds(row, groups), :] = jnp.concatenate(grouped, axis=0)
    pairs = ((edges, grad_one), (act_one_ref[...], grad_two_ref[...]), (act_two, grad_upd))
    for at, (left, right) in enumerate(pairs):
        terms[pl.ds(at * width, width), :] += dot_rows(left, right)

    @pl.when(step == pl.num_programs(0) - 1)
    def _():
        agg = aggregate[...].astype(bf16)
        node_out_ref[...] = (node_ref[...].astype(f32) + dot(agg, w_node_ref[...])).astype(bf16)
        src = grad_src[...].astype(bf16)
        grad_node_ref[...] = node_cot_ref[...].astype(f32) + dot_turned(src, w_src_ref[...])
        early_ref[pl.ds(0, deep), :] = dot_rows(node_ref[...], src).astype(bf16)
        early_ref[pl.ds(deep, 3 * width), :] = terms[...].astype(bf16)
        low = deep + 3 * width
        for at in range(0, deep, width):
            slab = dot_rows(agg, node_cot_ref[:, pl.ds(at, width)])
            early_ref[pl.ds(low + at, width), :] = slab.astype(bf16)
        low = low + deep
        rest = early_ref.shape[0] - low
        early_ref[pl.ds(low, rest), :] = jnp.zeros((rest, width), bf16)


def edge_side(
    edges, cots, mask, chain, node_in, node_cot, w_src, w_one, w_three, w_node, early_rows
):
    total, width = edges.shape
    nodes, nbrs = mask.shape
    rest = tuple(map(in_hbm, (node_in, node_cot, w_src, w_one, w_three, w_node)))
    deep = node_in.shape[1]
    f32, bf16 = jnp.float32, jnp.bfloat16
    rows = pl.BlockSpec((SIDE_BLOCK, width), lambda i: (i, 0))
    masks = pl.BlockSpec((SIDE_BLOCK // nbrs, nbrs), lambda i: (i, 0))
    square = whole(width, width)
    small = pltpu.VMEM((nodes, width), f32)
    return pl.pallas_call(
        functools.partial(side_body, 1.0 / math.sqrt(nbrs)),
        grid=(total // SIDE_BLOCK,),
        in_specs=[rows, rows, masks] + [rows] * 4 + [whole(nodes, deep), whole(nodes, deep)]
        + [whole(deep, width), square, square, whole(width, deep)],
        out_specs=[rows, rows, whole(early_rows, width), whole(nodes, deep), whole(nodes, deep)],
        scratch_shapes=[small, small, small, pltpu.VMEM((3 * width, width), f32)],
        out_shape=[pltpu.HBM((total, width), bf16)] * 2
        + [pltpu.HBM((early_rows, width), bf16)]
        + [pltpu.HBM((nodes, deep), bf16), pltpu.HBM((nodes, deep), f32)],
        compiler_params=pltpu.CompilerParams(vmem_limit_bytes=24 * 1024 * 1024),
        cost_estimate=pl.CostEstimate(
            flops=10 * total * width * width, bytes_accessed=24 * 2**20, transcendentals=0
        ),
        name="edge_side",
    )(*map(in_hbm, (edges, cots)), in_hbm(mask), *map(in_hbm, chain), *rest)


def meet_body(arriving_ref, node_ref, early_ref, partial_ref, message_ref):
    blocks, share, width = arriving_ref.shape
    bf16, f32 = jnp.bfloat16, jnp.float32
    value = arriving_ref[0].astype(f32)
    for at in range(1, blocks):
        value = value + arriving_ref[at].astype(f32)
    partial = value.astype(bf16)
    partial_ref[...] = partial
    late = dot_rows(node_ref[...], partial).astype(bf16)
    rest = late.shape[0] // blocks
    extra = early_ref.shape[0] // blocks
    for at in range(blocks):
        message_ref[at, pl.ds(0, extra), :] = early_ref[pl.ds(at * extra, extra), :]
        message_ref[at, pl.ds(extra, rest), :] = late[at * rest : (at + 1) * rest]


def meet(arriving, node_column, early, late_rows):
    blocks, share, width = arriving.shape
    deep = late_rows
    height = (early.shape[0] + deep) // blocks
    return pl.pallas_call(
        meet_body,
        grid=(1,),
        in_specs=[whole(*arriving.shape), whole(share, deep), whole(*early.shape)],
        out_specs=[whole(share, width), whole(blocks, height, width)],
        out_shape=[
            jax.ShapeDtypeStruct((share, width), jnp.bfloat16),
            jax.ShapeDtypeStruct((blocks, height, width), jnp.bfloat16),
        ],
        compiler_params=pltpu.CompilerParams(vmem_limit_bytes=24 * 1024 * 1024),
        cost_estimate=pl.CostEstimate(
            flops=2 * share * deep * width, bytes_accessed=4 * 2**20, transcendentals=0
        ),
        name="meet",
    )(arriving, in_hbm(node_column), in_hbm(early))


def finish_body(node_scale, edge_scale, sums_ref, src_ref, dst_ref, one_ref, two_ref, three_ref, node_ref):
    blocks, height, width = sums_ref.shape
    deep = src_ref.shape[0]
    piece = deep // blocks
    extra = height - piece
    for at in range(blocks):
        late = sums_ref[at, pl.ds(extra, piece), :].astype(jnp.float32)
        dst_ref[pl.ds(at * piece, piece), :] = late * node_scale
    squares = (one_ref, two_ref, three_ref)
    for low in range(0, 2 * deep + 3 * width, piece):
        at, place = low // extra, low % extra
        value = sums_ref[at, pl.ds(place, piece), :].astype(jnp.float32)
        if low < deep:
            src_ref[pl.ds(low, piece), :] = value * node_scale
        elif low < deep + 3 * width:
            which, row = (low - deep) // width, (low - deep) % width
            squares[which][pl.ds(row, piece), :] = value * edge_scale
        else:
            slab, row = (low - deep - 3 * width) // width, (low - deep - 3 * width) % width
            node_ref[pl.ds(row, piece), pl.ds(slab * width, width)] = value * node_scale


def finish(sums, deep, node_scale, edge_scale):
    width = sums.shape[2]
    shapes = [(deep, width)] * 2 + [(width, width)] * 3 + [(width, deep)]
    return pl.pallas_call(
        functools.partial(finish_body, node_scale, edge_scale),
        grid=(1,),
        in_specs=[whole(*sums.shape)],
        out_specs=[whole(*shape) for shape in shapes],
        out_shape=[jax.ShapeDtypeStruct(shape, jnp.float32) for shape in shapes],
        name="finish",
    )(sums)


def shards(
    node_in,
    edge_in,
    neighbours,
    edge_mask,
    w_src,
    w_dst,
    w_edge_one,
    w_edge_two,
    w_edge_three,
    w_node,
    node_cot,
    edge_cot,
):
    row_count, nbr_count, width = edge_in.shape
    deep = node_in.shape[1]
    bf16, f32 = jnp.bfloat16, jnp.float32
    long, tall, wide = lax.axis_size("z"), lax.axis_size("y"), lax.axis_size("x")
    blocks = wide * tall
    total = blocks * long * row_count
    node_scale = 1.0 / math.sqrt(total)
    edge_scale = 1.0 / math.sqrt(total * nbr_count)

    proj = dot(node_in, w_dst).astype(bf16)
    column = spread(jnp.concatenate([node_in, proj], axis=1), RING).reshape(-1, deep + width)
    own_row, rest = neighbours % row_count, neighbours // row_count
    at_x, rest = rest % wide, rest // wide
    places = ((at_x * (tall * long) + rest) * row_count + own_row).reshape(-1)
    column, places = lax.optimization_barrier((column, places))
    table = spread(column[:, deep:], PLANE).reshape(total, width)
    edges = edge_in.reshape(row_count * nbr_count, width)
    cots = edge_cot.reshape(row_count * nbr_count, width)
    base, up = edge_prep(
        edges, cots, edge_mask, node_in, node_cot, w_src, w_edge_one, w_edge_three, w_node
    )
    table, base, up = lax.optimization_barrier((table, base, up))
    *chain, message = edge_chain(places, table, base, up, w_edge_two)
    *chain, message = lax.optimization_barrier((*chain, message))
    arriving = exchange(message.reshape(blocks, -1, width), PLANE)
    extra = -(-(2 * deep + 3 * width) // (blocks * 16)) * 16
    edge_out, grad_edge, early, node_out, grad_node = edge_side(
        edges,
        cots,
        edge_mask,
        chain,
        node_in,
        node_cot,
        w_src,
        w_edge_one,
        w_edge_three,
        w_node,
        blocks * extra,
    )
    partial, message = meet(arriving, column, early, deep)
    weights = sum_first(exchange(message, PLANE)).astype(bf16)
    weights = jnp.broadcast_to(weights[None], (long, *weights.shape))
    packed = jnp.concatenate([partial.reshape(long, row_count, width), weights], axis=1)
    own = sum_first(exchange(packed, RING)).astype(bf16)
    grad_node = (grad_node + dot_turned(own[:row_count], w_dst)).astype(bf16)
    weights = finish(spread(own[row_count:], PLANE), deep, node_scale, edge_scale)
    return (
        node_out,
        edge_out.reshape(edge_in.shape),
        grad_node,
        grad_edge.reshape(edge_in.shape),
        *weights,
    )


def solution(mesh):
    shape = mesh.shape
    outer = shape["node"]
    inner = outer
    devices = mesh.devices.reshape(shape["cplx"], outer, shape["edge"] // inner, inner)
    mesh = Mesh(devices, ("cplx", *ALL))
    in_specs = (
        P(("cplx", *ALL), None),
        P(("cplx", *ALL), None, None),
        P(("cplx", *ALL), None),
        P(("cplx", *ALL), None),
        P(),
        P(),
        P(),
        P(),
        P(),
        P(),
        P(("cplx", *ALL), None),
        P(("cplx", *ALL), None, None),
    )
    out_specs = (
        P(("cplx", *ALL), None),
        P(("cplx", *ALL), None, None),
        P(("cplx", *ALL), None),
        P(("cplx", *ALL), None, None),
        P("cplx", None),
        P("cplx", None),
        P("cplx", None),
        P("cplx", None),
        P("cplx", None),
        P("cplx", None),
    )
    return jax.shard_map(shards, mesh=mesh, in_specs=in_specs, out_specs=out_specs, check_vma=False)
```

```python
import functools
import math

import jax
import jax.numpy as jnp
from jax import lax
from jax.experimental import pallas as pl
from jax.experimental.pallas import tpu as pltpu
from jax.sharding import Mesh
from jax.sharding import PartitionSpec as P

RING = ("z",)
PLANE = ("x", "y")
ALL = ("y", "z", "x")
SUMS = 4
BLOCK = 1024
CHUNKS = 4
SIDE_BLOCK = 1024
PIECE = 512


def exchange(value, axes):
    return lax.all_to_all(value, axes, 0, 0, tiled=True)


def spread(value, axes):
    count = math.prod(lax.axis_size(axis) for axis in axes)
    return exchange(jnp.broadcast_to(value[None], (count, *value.shape)), axes)


def sum_first(value):
    return jnp.sum(value.astype(jnp.float32), axis=0)


def sigmoid(value):
    return 0.5 * jnp.tanh(0.5 * value) + 0.5


def deriv(value, sigma_val):
    return sigma_val * (1.0 + value * (1.0 - sigma_val))


def dot(left, right):
    return jnp.dot(left, right, preferred_element_type=jnp.float32)


def dot_turned(left, right):
    return lax.dot_general(
        left, right, (((1,), (1,)), ((), ())), preferred_element_type=jnp.float32
    )


def dot_rows(left, right):
    return lax.dot_general(
        left, right, (((0,), (0,)), ((), ())), preferred_element_type=jnp.float32
    )


def rows_of(values, count):
    width = values.shape[1]
    rows = [jnp.broadcast_to(values[j : j + 1, :], (count, width)) for j in range(values.shape[0])]
    return jnp.concatenate(rows, axis=0)


def mask_of(mask, width):
    turned = mask.astype(jnp.float32).T
    count = turned.shape[0]
    columns = [jnp.broadcast_to(turned[:, j : j + 1], (count, width)) for j in range(mask.shape[0])]
    return jnp.concatenate(columns, axis=0)


def prep_body(
    agg_scale,
    edge_ref,
    cot_ref,
    mask_ref,
    node_ref,
    node_cot_ref,
    w_src_ref,
    one_ref,
    three_ref,
    w_node_ref,
    base_ref,
    up_ref,
    src_proj,
    grad_agg,
):
    step = pl.program_id(0)
    groups, nbrs = mask_ref.shape
    width = edge_ref.shape[1]
    bf16, f32 = jnp.bfloat16, jnp.float32

    @pl.when(step == 0)
    def _():
        src_proj[...] = dot(node_ref[...], w_src_ref[...]).astype(bf16).astype(f32)
        grad_agg[...] = dot_turned(node_cot_ref[...], w_node_ref[...]) * agg_scale

    row = pl.multiple_of(step * groups, groups)
    masked = mask_of(mask_ref[...], width)
    agg_rows = rows_of(grad_agg[pl.ds(row, groups), :], nbrs)
    grad_upd = (masked * (cot_ref[...].astype(f32) + masked * agg_rows)).astype(bf16)
    up_ref[...] = dot_turned(grad_upd, three_ref[...])
    src_rows = rows_of(src_proj[pl.ds(row, groups), :], nbrs)
    base_ref[...] = dot(edge_ref[...], one_ref[...]) + src_rows


def in_hbm(value):
    return pltpu.with_memory_space_constraint(value, pltpu.HBM)


def whole(*shape):
    return pl.BlockSpec(shape, lambda i, *places: (0,) * len(shape))


def edge_prep(edges, cots, mask, node_in, node_cot, w_src, w_one, w_three, w_node):
    total, width = edges.shape
    nodes, nbrs = mask.shape
    deep = node_in.shape[1]
    rest = (edges, cots, mask, node_in, node_cot, w_src, w_one, w_three, w_node)
    rows = pl.BlockSpec((SIDE_BLOCK, width), lambda i: (i, 0))
    masks = pl.BlockSpec((SIDE_BLOCK // nbrs, nbrs), lambda i: (i, 0))
    square = whole(width, width)
    small = pltpu.VMEM((nodes, width), jnp.float32)
    return pl.pallas_call(
        functools.partial(prep_body, 1.0 / math.sqrt(nbrs)),
        grid=(total // SIDE_BLOCK,),
        in_specs=[rows, rows, masks, whole(nodes, deep), whole(nodes, deep), whole(deep, width)]
        + [square, square, whole(width, deep)],
        out_specs=[rows, rows],
        scratch_shapes=[small, small],
        out_shape=[pltpu.HBM((total, width), jnp.float32)] * 2,
        compiler_params=pltpu.CompilerParams(vmem_limit_bytes=24 * 1024 * 1024),
        cost_estimate=pl.CostEstimate(
            flops=4 * total * width * width, bytes_accessed=12 * 2**20, transcendentals=0
        ),
        name="edge_prep",
    )(*map(in_hbm, rest))


def chain_body(
    place_ref,
    table_ref,
    base_ref,
    up_ref,
    two_ref,
    act_one_ref,
    act_two_ref,
    grad_two_ref,
    grad_one_ref,
    message_ref,
    table,
    *held,
):
    step = pl.program_id(0)
    count, width = table.shape
    block = base_ref.shape[0]
    chunk = block // CHUNKS
    sums, pulled, grads = held[:SUMS], held[SUMS : SUMS + CHUNKS], held[SUMS + CHUNKS :]
    bf16, f32 = jnp.bfloat16, jnp.float32

    @pl.when(step == 0)
    def _():
        def fill(at, carry):
            rows = pl.ds(pl.multiple_of(at * PIECE, PIECE), PIECE)
            table[rows, :] = table_ref[rows, :].astype(f32)
            for one in sums:
                one[rows, :] = jnp.zeros((PIECE, width), f32)
            return carry

        lax.fori_loop(0, count // PIECE, fill, 0)

    first = step * block

    def pull(at):
        for k in range(chunk):
            place = place_ref[first + at * chunk + k]
            pulled[at][pl.ds(k, 1), :] = table[pl.ds(place, 1), :]

    def push(at):
        for k in range(chunk):
            one = sums[k % SUMS]
            place = pl.ds(place_ref[first + at * chunk + k], 1)
            one[place, :] += grads[at][pl.ds(k, 1), :]

    def work(at):
        span = pl.ds(at * chunk, chunk)
        pre_one = base_ref[span, :] + pulled[at][...]
        sigma_one = sigmoid(pre_one)
        act_one = (pre_one * sigma_one).astype(bf16)
        act_one_ref[span, :] = act_one
        pre_two = dot(act_one, two_ref[...])
        sigma_two = sigmoid(pre_two)
        act_two_ref[span, :] = (pre_two * sigma_two).astype(bf16)
        grad_two = (up_ref[span, :] * deriv(pre_two, sigma_two)).astype(bf16)
        grad_two_ref[span, :] = grad_two
        grad_one = (dot_turned(grad_two, two_ref[...]) * deriv(pre_one, sigma_one)).astype(bf16)
        grad_one_ref[span, :] = grad_one
        grads[at][...] = grad_one.astype(f32)

    pull(0)
    for at in range(CHUNKS):
        if at + 1 < CHUNKS:
            pull(at + 1)
        work(at)
        if at > 0:
            push(at - 1)
    push(CHUNKS - 1)

    @pl.when(step == pl.num_programs(0) - 1)
    def _():
        def merge(at, carry):
            rows = pl.ds(pl.multiple_of(at * PIECE, PIECE), PIECE)
            value = sums[0][rows, :]
            for one in sums[1:]:
                value = value + one[rows, :]
            message_ref[rows, :] = value.astype(bf16)
            return carry

        lax.fori_loop(0, count // PIECE, merge, 0)


def edge_chain(places, table, base, up, w_two):
    count, width = table.shape
    total = places.shape[0]
    f32, bf16 = jnp.float32, jnp.bfloat16
    rows = pl.BlockSpec((BLOCK, width), lambda i, places: (i, 0))
    held = pltpu.VMEM((count, width), f32)
    part = pltpu.VMEM((BLOCK // CHUNKS, width), f32)
    return pl.pallas_call(
        chain_body,
        grid_spec=pltpu.PrefetchScalarGridSpec(
            num_scalar_prefetch=1,
            grid=(total // BLOCK,),
            in_specs=[pl.BlockSpec(memory_space=pltpu.VMEM), rows, rows, whole(width, width)],
            out_specs=[rows] * 4 + [whole(count, width)],
            scratch_shapes=[held] + [held] * SUMS + [part] * (2 * CHUNKS),
        ),
        out_shape=[pltpu.HBM((total, width), bf16)] * 4 + [pltpu.HBM((count, width), bf16)],
        compiler_params=pltpu.CompilerParams(vmem_limit_bytes=44 * 1024 * 1024),
        cost_estimate=pl.CostEstimate(
            flops=8 * total * width * width, bytes_accessed=12 * 2**20, transcendentals=0
        ),
        name="edge_chain",
    )(places, table, in_hbm(base), in_hbm(up), in_hbm(w_two))


def side_body(
    agg_scale,
    edge_ref,
    cot_ref,
    mask_ref,
    act_one_ref,
    act_two_ref,
    grad_two_ref,
    grad_one_ref,
    node_ref,
    node_cot_ref,
    w_src_ref,
    one_ref,
    three_ref,
    w_node_ref,
    edge_out_ref,
    grad_edge_ref,
    early_ref,
    node_out_ref,
    grad_node_ref,
    grad_agg,
    aggregate,
    grad_src,
    terms,
):
    step = pl.program_id(0)
    groups, nbrs = mask_ref.shape
    width = edge_ref.shape[1]
    deep = node_ref.shape[1]
    bf16, f32 = jnp.bfloat16, jnp.float32

    @pl.when(step == 0)
    def _():
        terms[...] = jnp.zeros(terms.shape, f32)
        grad_agg[...] = dot_turned(node_cot_ref[...], w_node_ref[...]) * agg_scale

    row = pl.multiple_of(step * groups, groups)
    masked = mask_of(mask_ref[...], width)
    grad_new = cot_ref[...].astype(f32) + masked * rows_of(grad_agg[pl.ds(row, groups), :], nbrs)
    grad_upd = (masked * grad_new).astype(bf16)
    grad_one = grad_one_ref[...]
    grad_edge_ref[...] = (grad_new + dot_turned(grad_one, one_ref[...])).astype(bf16)
    edges = edge_ref[...]
    act_two = act_two_ref[...]
    edge_new = edges.astype(f32) + masked * dot(act_two, three_ref[...])
    edge_out_ref[...] = edge_new.astype(bf16)
    kept = masked * edge_new
    grad_wide = grad_one.astype(f32)
    added, grouped = [], []
    for j in range(groups):
        part = slice(j * nbrs, (j + 1) * nbrs)
        added.append(jnp.sum(kept[part], axis=0, keepdims=True))
        grouped.append(jnp.sum(grad_wide[part], axis=0, keepdims=True))
    aggregate[pl.ds(row, groups), :] = jnp.concatenate(added, axis=0) * agg_scale
    grad_src[pl.ds(row, groups), :] = jnp.concatenate(grouped, axis=0)
    pairs = ((edges, grad_one), (act_one_ref[...], grad_two_ref[...]), (act_two, grad_upd))
    for at, (left, right) in enumerate(pairs):
        terms[pl.ds(at * width, width), :] += dot_rows(left, right)

    @pl.when(step == pl.num_programs(0) - 1)
    def _():
        agg = aggregate[...].astype(bf16)
        node_out_ref[...] = (node_ref[...].astype(f32) + dot(agg, w_node_ref[...])).astype(bf16)
        src = grad_src[...].astype(bf16)
        grad_node_ref[...] = node_cot_ref[...].astype(f32) + dot_turned(src, w_src_ref[...])
        early_ref[pl.ds(0, deep), :] = dot_rows(node_ref[...], src).astype(bf16)
        early_ref[pl.ds(deep, 3 * width), :] = terms[...].astype(bf16)
        low = deep + 3 * width
        for at in range(0, deep, width):
            slab = dot_rows(agg, node_cot_ref[:, pl.ds(at, width)])
            early_ref[pl.ds(low + at, width), :] = slab.astype(bf16)
        low = low + deep
        rest = early_ref.shape[0] - low
        early_ref[pl.ds(low, rest), :] = jnp.zeros((rest, width), bf16)


def edge_side(
    edges, cots, mask, chain, node_in, node_cot, w_src, w_one, w_three, w_node, early_rows
):
    total, width = edges.shape
    nodes, nbrs = mask.shape
    rest = tuple(map(in_hbm, (node_in, node_cot, w_src, w_one, w_three, w_node)))
    deep = node_in.shape[1]
    f32, bf16 = jnp.float32, jnp.bfloat16
    rows = pl.BlockSpec((SIDE_BLOCK, width), lambda i: (i, 0))
    masks = pl.BlockSpec((SIDE_BLOCK // nbrs, nbrs), lambda i: (i, 0))
    square = whole(width, width)
    small = pltpu.VMEM((nodes, width), f32)
    return pl.pallas_call(
        functools.partial(side_body, 1.0 / math.sqrt(nbrs)),
        grid=(total // SIDE_BLOCK,),
        in_specs=[rows, rows, masks] + [rows] * 4 + [whole(nodes, deep), whole(nodes, deep)]
        + [whole(deep, width), square, square, whole(width, deep)],
        out_specs=[rows, rows, whole(early_rows, width), whole(nodes, deep), whole(nodes, deep)],
        scratch_shapes=[small, small, small, pltpu.VMEM((3 * width, width), f32)],
        out_shape=[pltpu.HBM((total, width), bf16)] * 2
        + [pltpu.HBM((early_rows, width), bf16)]
        + [pltpu.HBM((nodes, deep), bf16), pltpu.HBM((nodes, deep), f32)],
        compiler_params=pltpu.CompilerParams(vmem_limit_bytes=24 * 1024 * 1024),
        cost_estimate=pl.CostEstimate(
            flops=10 * total * width * width, bytes_accessed=24 * 2**20, transcendentals=0
        ),
        name="edge_side",
    )(*map(in_hbm, (edges, cots)), in_hbm(mask), *map(in_hbm, chain), *rest)


def meet_body(turn_ref, arriving_ref, early_ref, *rest):
    *node_refs, partial_ref, message_ref = rest
    blocks, share, width = arriving_ref.shape
    count = len(node_refs)
    own = share // count
    bf16, f32 = jnp.bfloat16, jnp.float32
    value = arriving_ref[0].astype(f32)
    for at in range(1, blocks):
        value = value + arriving_ref[at].astype(f32)
    partial_ref[...] = value.astype(bf16)
    late = None
    for shift, node_ref in enumerate(node_refs):
        place = lax.rem(turn_ref[0] + (count - shift), count)
        rows = pl.ds(pl.multiple_of(place * own, own), own)
        term = dot_rows(node_ref[...], partial_ref[rows, :])
        late = term if late is None else late + term
    late = late.astype(bf16)
    piece = late.shape[0] // blocks
    extra = early_ref.shape[0] // blocks
    for at in range(blocks):
        message_ref[at, pl.ds(0, extra), :] = early_ref[pl.ds(at * extra, extra), :]
        message_ref[at, pl.ds(extra, piece), :] = late[at * piece : (at + 1) * piece]


def meet(turn, arriving, nodes, early):
    blocks, share, width = arriving.shape
    own, deep = nodes[0].shape
    height = (early.shape[0] + deep) // blocks
    return pl.pallas_call(
        meet_body,
        grid_spec=pltpu.PrefetchScalarGridSpec(
            num_scalar_prefetch=1,
            grid=(1,),
            in_specs=[whole(*arriving.shape), whole(*early.shape)] + [whole(own, deep)] * len(nodes),
            out_specs=[whole(share, width), whole(blocks, height, width)],
        ),
        out_shape=[
            jax.ShapeDtypeStruct((share, width), jnp.bfloat16),
            jax.ShapeDtypeStruct((blocks, height, width), jnp.bfloat16),
        ],
        compiler_params=pltpu.CompilerParams(vmem_limit_bytes=24 * 1024 * 1024),
        cost_estimate=pl.CostEstimate(
            flops=2 * share * deep * width, bytes_accessed=4 * 2**20, transcendentals=0
        ),
        name="meet",
    )(turn, arriving, in_hbm(early), *map(in_hbm, nodes))


def finish_body(node_scale, edge_scale, sums_ref, src_ref, dst_ref, one_ref, two_ref, three_ref, node_ref):
    blocks, height, width = sums_ref.shape
    deep = src_ref.shape[0]
    piece = deep // blocks
    extra = height - piece
    for at in range(blocks):
        late = sums_ref[at, pl.ds(extra, piece), :].astype(jnp.float32)
        dst_ref[pl.ds(at * piece, piece), :] = late * node_scale
    squares = (one_ref, two_ref, three_ref)
    for low in range(0, 2 * deep + 3 * width, piece):
        at, place = low // extra, low % extra
        value = sums_ref[at, pl.ds(place, piece), :].astype(jnp.float32)
        if low < deep:
            src_ref[pl.ds(low, piece), :] = value * node_scale
        elif low < deep + 3 * width:
            which, row = (low - deep) // width, (low - deep) % width
            squares[which][pl.ds(row, piece), :] = value * edge_scale
        else:
            slab, row = (low - deep - 3 * width) // width, (low - deep - 3 * width) % width
            node_ref[pl.ds(row, piece), pl.ds(slab * width, width)] = value * node_scale


def finish(sums, deep, node_scale, edge_scale):
    width = sums.shape[2]
    shapes = [(deep, width)] * 2 + [(width, width)] * 3 + [(width, deep)]
    return pl.pallas_call(
        functools.partial(finish_body, node_scale, edge_scale),
        grid=(1,),
        in_specs=[whole(*sums.shape)],
        out_specs=[whole(*shape) for shape in shapes],
        out_shape=[jax.ShapeDtypeStruct(shape, jnp.float32) for shape in shapes],
        name="finish",
    )(sums)


def shards(
    node_in,
    edge_in,
    neighbours,
    edge_mask,
    w_src,
    w_dst,
    w_edge_one,
    w_edge_two,
    w_edge_three,
    w_node,
    node_cot,
    edge_cot,
):
    row_count, nbr_count, width = edge_in.shape
    deep = node_in.shape[1]
    bf16, f32 = jnp.bfloat16, jnp.float32
    long, tall, wide = lax.axis_size("z"), lax.axis_size("y"), lax.axis_size("x")
    blocks = wide * tall
    total = blocks * long * row_count
    node_scale = 1.0 / math.sqrt(total)
    edge_scale = 1.0 / math.sqrt(total * nbr_count)

    column = spread(dot(node_in, w_dst).astype(bf16), RING)
    own_row, rest = neighbours % row_count, neighbours // row_count
    at_x, rest = rest % wide, rest // wide
    places = ((at_x * (tall * long) + rest) * row_count + own_row).reshape(-1)
    column, places, node_late = lax.optimization_barrier((column, places, node_in))
    table = spread(column.reshape(-1, width), PLANE).reshape(total, width)
    turns = [[(at, (at + shift) % long) for at in range(long)] for shift in range(long)]
    nodes = [node_in] + [lax.ppermute(node_late, "z", pairs) for pairs in turns[1 : long // 2]]
    edges = edge_in.reshape(row_count * nbr_count, width)
    cots = edge_cot.reshape(row_count * nbr_count, width)
    base, up = edge_prep(
        edges, cots, edge_mask, node_in, node_cot, w_src, w_edge_one, w_edge_three, w_node
    )
    half = long // 2
    table, base, up, *nodes = lax.optimization_barrier((table, base, up, *nodes))
    *chain, message = edge_chain(places, table, base, up, w_edge_two)
    *chain, message, node_late = lax.optimization_barrier((*chain, message, node_late))
    nodes += [lax.ppermute(node_late, "z", pairs) for pairs in turns[half:]]
    arriving = exchange(message.reshape(blocks, -1, width), PLANE)
    extra = -(-(2 * deep + 3 * width) // (blocks * 16)) * 16
    edge_out, grad_edge, early, node_out, grad_node = edge_side(
        edges,
        cots,
        edge_mask,
        chain,
        node_in,
        node_cot,
        w_src,
        w_edge_one,
        w_edge_three,
        w_node,
        blocks * extra,
    )
    arriving, early, *nodes = lax.optimization_barrier((arriving, early, *nodes))
    turn = jnp.full((1,), lax.axis_index("z"), jnp.int32)
    partial, message = meet(turn, arriving, nodes, early)
    weights = sum_first(exchange(message, PLANE)).astype(bf16)
    weights = jnp.broadcast_to(weights[None], (long, *weights.shape))
    packed = jnp.concatenate([partial.reshape(long, row_count, width), weights], axis=1)
    own = sum_first(exchange(packed, RING)).astype(bf16)
    grad_node = (grad_node + dot_turned(own[:row_count], w_dst)).astype(bf16)
    weights = finish(spread(own[row_count:], PLANE), deep, node_scale, edge_scale)
    return (
        node_out,
        edge_out.reshape(edge_in.shape),
        grad_node,
        grad_edge.reshape(edge_in.shape),
        *weights,
    )


def solution(mesh):
    shape = mesh.shape
    outer = shape["node"]
    inner = outer
    devices = mesh.devices.reshape(shape["cplx"], outer, shape["edge"] // inner, inner)
    mesh = Mesh(devices, ("cplx", *ALL))
    in_specs = (
        P(("cplx", *ALL), None),
        P(("cplx", *ALL), None, None),
        P(("cplx", *ALL), None),
        P(("cplx", *ALL), None),
        P(),
        P(),
        P(),
        P(),
        P(),
        P(),
        P(("cplx", *ALL), None),
        P(("cplx", *ALL), None, None),
    )
    out_specs = (
        P(("cplx", *ALL), None),
        P(("cplx", *ALL), None, None),
        P(("cplx", *ALL), None),
        P(("cplx", *ALL), None, None),
        P("cplx", None),
        P("cplx", None),
        P("cplx", None),
        P("cplx", None),
        P("cplx", None),
        P("cplx", None),
    )
    return jax.shard_map(shards, mesh=mesh, in_specs=in_specs, out_specs=out_specs, check_vma=False)
```

```python
import functools
import math

import jax
import jax.numpy as jnp
from jax import lax
from jax.experimental import pallas as pl
from jax.experimental.pallas import tpu as pltpu
from jax.sharding import Mesh
from jax.sharding import PartitionSpec as P

RING = ("z",)
PLANE = ("x", "y")
ALL = ("y", "z", "x")
SUMS = 4
BLOCK = 1024
CHUNKS = 8
SIDE_BLOCK = 1024
PIECE = 512


def exchange(value, axes):
    return lax.all_to_all(value, axes, 0, 0, tiled=True)


def spread(value, axes):
    count = math.prod(lax.axis_size(axis) for axis in axes)
    return exchange(jnp.broadcast_to(value[None], (count, *value.shape)), axes)


def sum_first(value):
    return jnp.sum(value.astype(jnp.float32), axis=0)


def sigmoid(value):
    return 0.5 * jnp.tanh(0.5 * value) + 0.5


def deriv(value, sigma_val):
    return sigma_val * (1.0 + value * (1.0 - sigma_val))


def dot(left, right):
    return jnp.dot(left, right, preferred_element_type=jnp.float32)


def dot_turned(left, right):
    return lax.dot_general(
        left, right, (((1,), (1,)), ((), ())), preferred_element_type=jnp.float32
    )


def dot_rows(left, right):
    return lax.dot_general(
        left, right, (((0,), (0,)), ((), ())), preferred_element_type=jnp.float32
    )


def rows_of(values, count):
    width = values.shape[1]
    rows = [jnp.broadcast_to(values[j : j + 1, :], (count, width)) for j in range(values.shape[0])]
    return jnp.concatenate(rows, axis=0)


def mask_of(mask, width):
    turned = mask.astype(jnp.float32).T
    count = turned.shape[0]
    columns = [jnp.broadcast_to(turned[:, j : j + 1], (count, width)) for j in range(mask.shape[0])]
    return jnp.concatenate(columns, axis=0)


def project_body(node_ref, weight_ref, out_ref):
    value = dot(node_ref[...], weight_ref[...]).astype(jnp.bfloat16)
    for at in range(out_ref.shape[0]):
        out_ref[at] = value


def whole(*shape):
    return pl.BlockSpec(shape, lambda i, *places: (0,) * len(shape))


def in_hbm(value):
    return pltpu.with_memory_space_constraint(value, pltpu.HBM)


def project(node_in, weight, count):
    nodes, width = node_in.shape[0], weight.shape[1]
    return pl.pallas_call(
        project_body,
        grid=(1,),
        in_specs=[whole(*node_in.shape), whole(*weight.shape)],
        out_specs=whole(count, nodes, width),
        out_shape=pltpu.HBM((count, nodes, width), jnp.bfloat16),
        compiler_params=pltpu.CompilerParams(vmem_limit_bytes=8 * 1024 * 1024),
        name="project",
    )(in_hbm(node_in), in_hbm(weight))


def prep_body(
    agg_scale,
    edge_ref,
    cot_ref,
    mask_ref,
    node_ref,
    node_cot_ref,
    w_src_ref,
    one_ref,
    three_ref,
    w_node_ref,
    base_ref,
    up_ref,
    src_proj,
    grad_agg,
):
    step = pl.program_id(0)
    groups, nbrs = mask_ref.shape
    width = edge_ref.shape[1]
    bf16, f32 = jnp.bfloat16, jnp.float32

    @pl.when(step == 0)
    def _():
        src_proj[...] = dot(node_ref[...], w_src_ref[...]).astype(bf16).astype(f32)
        grad_agg[...] = dot_turned(node_cot_ref[...], w_node_ref[...]) * agg_scale

    row = pl.multiple_of(step * groups, groups)
    masked = mask_of(mask_ref[...], width)
    agg_rows = rows_of(grad_agg[pl.ds(row, groups), :], nbrs)
    grad_upd = (masked * (cot_ref[...].astype(f32) + masked * agg_rows)).astype(bf16)
    up_ref[...] = dot_turned(grad_upd, three_ref[...])
    src_rows = rows_of(src_proj[pl.ds(row, groups), :], nbrs)
    base_ref[...] = dot(edge_ref[...], one_ref[...]) + src_rows


def edge_prep(edges, cots, mask, node_in, node_cot, w_src, w_one, w_three, w_node):
    total, width = edges.shape
    nodes, nbrs = mask.shape
    deep = node_in.shape[1]
    rest = (edges, cots, mask, node_in, node_cot, w_src, w_one, w_three, w_node)
    rows = pl.BlockSpec((SIDE_BLOCK, width), lambda i: (i, 0))
    masks = pl.BlockSpec((SIDE_BLOCK // nbrs, nbrs), lambda i: (i, 0))
    square = whole(width, width)
    small = pltpu.VMEM((nodes, width), jnp.float32)
    return pl.pallas_call(
        functools.partial(prep_body, 1.0 / math.sqrt(nbrs)),
        grid=(total // SIDE_BLOCK,),
        in_specs=[rows, rows, masks, whole(nodes, deep), whole(nodes, deep), whole(deep, width)]
        + [square, square, whole(width, deep)],
        out_specs=[rows, rows],
        scratch_shapes=[small, small],
        out_shape=[pltpu.HBM((total, width), jnp.float32)] * 2,
        compiler_params=pltpu.CompilerParams(vmem_limit_bytes=24 * 1024 * 1024),
        cost_estimate=pl.CostEstimate(
            flops=4 * total * width * width, bytes_accessed=12 * 2**20, transcendentals=0
        ),
        name="edge_prep",
    )(*map(in_hbm, rest))


def chain_body(
    place_ref,
    table_ref,
    base_ref,
    up_ref,
    two_ref,
    act_one_ref,
    act_two_ref,
    grad_two_ref,
    grad_one_ref,
    message_ref,
    table,
    *held,
):
    step = pl.program_id(0)
    count, width = table.shape
    block = base_ref.shape[0]
    chunk = block // CHUNKS
    sums, pulled, grads = held[:SUMS], held[SUMS : SUMS + CHUNKS], held[SUMS + CHUNKS :]
    bf16, f32 = jnp.bfloat16, jnp.float32

    @pl.when(step == 0)
    def _():
        def fill(at, carry):
            rows = pl.ds(pl.multiple_of(at * PIECE, PIECE), PIECE)
            table[rows, :] = table_ref[rows, :].astype(f32)
            for one in sums:
                one[rows, :] = jnp.zeros((PIECE, width), f32)
            return carry

        lax.fori_loop(0, count // PIECE, fill, 0)

    first = step * block

    def pull(at):
        for k in range(chunk):
            place = place_ref[first + at * chunk + k]
            pulled[at][pl.ds(k, 1), :] = table[pl.ds(place, 1), :]

    def push(at):
        for k in range(chunk):
            one = sums[k % SUMS]
            place = pl.ds(place_ref[first + at * chunk + k], 1)
            one[place, :] += grads[at][pl.ds(k, 1), :]

    def work(at):
        span = pl.ds(at * chunk, chunk)
        pre_one = base_ref[span, :] + pulled[at][...]
        sigma_one = sigmoid(pre_one)
        act_one = (pre_one * sigma_one).astype(bf16)
        act_one_ref[span, :] = act_one
        pre_two = dot(act_one, two_ref[...])
        sigma_two = sigmoid(pre_two)
        act_two_ref[span, :] = (pre_two * sigma_two).astype(bf16)
        grad_two = (up_ref[span, :] * deriv(pre_two, sigma_two)).astype(bf16)
        grad_two_ref[span, :] = grad_two
        grad_one = (dot_turned(grad_two, two_ref[...]) * deriv(pre_one, sigma_one)).astype(bf16)
        grad_one_ref[span, :] = grad_one
        grads[at][...] = grad_one.astype(f32)

    pull(0)
    for at in range(CHUNKS):
        if at + 1 < CHUNKS:
            pull(at + 1)
        work(at)
        if at > 0:
            push(at - 1)
    push(CHUNKS - 1)

    @pl.when(step == pl.num_programs(0) - 1)
    def _():
        def merge(at, carry):
            rows = pl.ds(pl.multiple_of(at * PIECE, PIECE), PIECE)
            value = sums[0][rows, :]
            for one in sums[1:]:
                value = value + one[rows, :]
            message_ref[rows, :] = value.astype(bf16)
            return carry

        lax.fori_loop(0, count // PIECE, merge, 0)


def edge_chain(places, table, base, up, w_two):
    count, width = table.shape
    total = places.shape[0]
    f32, bf16 = jnp.float32, jnp.bfloat16
    rows = pl.BlockSpec((BLOCK, width), lambda i, places: (i, 0))
    held = pltpu.VMEM((count, width), f32)
    part = pltpu.VMEM((BLOCK // CHUNKS, width), f32)
    return pl.pallas_call(
        chain_body,
        grid_spec=pltpu.PrefetchScalarGridSpec(
            num_scalar_prefetch=1,
            grid=(total // BLOCK,),
            in_specs=[pl.BlockSpec(memory_space=pltpu.VMEM), rows, rows, whole(width, width)],
            out_specs=[rows] * 4 + [whole(count, width)],
            scratch_shapes=[held] + [held] * SUMS + [part] * (2 * CHUNKS),
        ),
        out_shape=[pltpu.HBM((total, width), bf16)] * 4 + [pltpu.HBM((count, width), bf16)],
        compiler_params=pltpu.CompilerParams(vmem_limit_bytes=44 * 1024 * 1024),
        cost_estimate=pl.CostEstimate(
            flops=8 * total * width * width, bytes_accessed=12 * 2**20, transcendentals=0
        ),
        name="edge_chain",
    )(places, table, in_hbm(base), in_hbm(up), in_hbm(w_two))


def side_body(
    agg_scale,
    edge_ref,
    cot_ref,
    mask_ref,
    act_one_ref,
    act_two_ref,
    grad_two_ref,
    grad_one_ref,
    node_ref,
    node_cot_ref,
    w_src_ref,
    one_ref,
    three_ref,
    w_node_ref,
    edge_out_ref,
    grad_edge_ref,
    early_ref,
    node_out_ref,
    grad_node_ref,
    grad_agg,
    aggregate,
    grad_src,
    terms,
):
    step = pl.program_id(0)
    groups, nbrs = mask_ref.shape
    width = edge_ref.shape[1]
    deep = node_ref.shape[1]
    bf16, f32 = jnp.bfloat16, jnp.float32

    @pl.when(step == 0)
    def _():
        terms[...] = jnp.zeros(terms.shape, f32)
        grad_agg[...] = dot_turned(node_cot_ref[...], w_node_ref[...]) * agg_scale

    row = pl.multiple_of(step * groups, groups)
    masked = mask_of(mask_ref[...], width)
    grad_new = cot_ref[...].astype(f32) + masked * rows_of(grad_agg[pl.ds(row, groups), :], nbrs)
    grad_upd = (masked * grad_new).astype(bf16)
    grad_one = grad_one_ref[...]
    grad_edge_ref[...] = (grad_new + dot_turned(grad_one, one_ref[...])).astype(bf16)
    edges = edge_ref[...]
    act_two = act_two_ref[...]
    edge_new = edges.astype(f32) + masked * dot(act_two, three_ref[...])
    edge_out_ref[...] = edge_new.astype(bf16)
    kept = masked * edge_new
    grad_wide = grad_one.astype(f32)
    added, grouped = [], []
    for j in range(groups):
        part = slice(j * nbrs, (j + 1) * nbrs)
        added.append(jnp.sum(kept[part], axis=0, keepdims=True))
        grouped.append(jnp.sum(grad_wide[part], axis=0, keepdims=True))
    aggregate[pl.ds(row, groups), :] = jnp.concatenate(added, axis=0) * agg_scale
    grad_src[pl.ds(row, groups), :] = jnp.concatenate(grouped, axis=0)
    pairs = ((edges, grad_one), (act_one_ref[...], grad_two_ref[...]), (act_two, grad_upd))
    for at, (left, right) in enumerate(pairs):
        terms[pl.ds(at * width, width), :] += dot_rows(left, right)

    @pl.when(step == pl.num_programs(0) - 1)
    def _():
        agg = aggregate[...].astype(bf16)
        node_out_ref[...] = (node_ref[...].astype(f32) + dot(agg, w_node_ref[...])).astype(bf16)
        src = grad_src[...].astype(bf16)
        grad_node_ref[...] = node_cot_ref[...].astype(f32) + dot_turned(src, w_src_ref[...])
        early_ref[pl.ds(0, deep), :] = dot_rows(node_ref[...], src).astype(bf16)
        early_ref[pl.ds(deep, 3 * width), :] = terms[...].astype(bf16)
        low = deep + 3 * width
        for at in range(0, deep, width):
            slab = dot_rows(agg, node_cot_ref[:, pl.ds(at, width)])
            early_ref[pl.ds(low + at, width), :] = slab.astype(bf16)
        low = low + deep
        rest = early_ref.shape[0] - low
        early_ref[pl.ds(low, rest), :] = jnp.zeros((rest, width), bf16)


def edge_side(
    edges, cots, mask, chain, node_in, node_cot, w_src, w_one, w_three, w_node, early_rows
):
    total, width = edges.shape
    nodes, nbrs = mask.shape
    rest = tuple(map(in_hbm, (node_in, node_cot, w_src, w_one, w_three, w_node)))
    deep = node_in.shape[1]
    f32, bf16 = jnp.float32, jnp.bfloat16
    rows = pl.BlockSpec((SIDE_BLOCK, width), lambda i: (i, 0))
    masks = pl.BlockSpec((SIDE_BLOCK // nbrs, nbrs), lambda i: (i, 0))
    square = whole(width, width)
    small = pltpu.VMEM((nodes, width), f32)
    return pl.pallas_call(
        functools.partial(side_body, 1.0 / math.sqrt(nbrs)),
        grid=(total // SIDE_BLOCK,),
        in_specs=[rows, rows, masks] + [rows] * 4 + [whole(nodes, deep), whole(nodes, deep)]
        + [whole(deep, width), square, square, whole(width, deep)],
        out_specs=[rows, rows, whole(early_rows, width), whole(nodes, deep), whole(nodes, deep)],
        scratch_shapes=[small, small, small, pltpu.VMEM((3 * width, width), f32)],
        out_shape=[pltpu.HBM((total, width), bf16)] * 2
        + [pltpu.HBM((early_rows, width), bf16)]
        + [pltpu.HBM((nodes, deep), bf16), pltpu.HBM((nodes, deep), f32)],
        compiler_params=pltpu.CompilerParams(vmem_limit_bytes=24 * 1024 * 1024),
        cost_estimate=pl.CostEstimate(
            flops=10 * total * width * width, bytes_accessed=24 * 2**20, transcendentals=0
        ),
        name="edge_side",
    )(*map(in_hbm, (edges, cots)), in_hbm(mask), *map(in_hbm, chain), *rest)


def meet_body(turn_ref, arriving_ref, early_ref, *rest):
    *node_refs, partial_ref, message_ref = rest
    blocks, share, width = arriving_ref.shape
    count = len(node_refs)
    own = share // count
    bf16, f32 = jnp.bfloat16, jnp.float32
    value = arriving_ref[0].astype(f32)
    for at in range(1, blocks):
        value = value + arriving_ref[at].astype(f32)
    partial_ref[...] = value.astype(bf16)
    late = None
    for shift, node_ref in enumerate(node_refs):
        place = lax.rem(turn_ref[0] + (count - shift), count)
        rows = pl.ds(pl.multiple_of(place * own, own), own)
        term = dot_rows(node_ref[...], partial_ref[rows, :])
        late = term if late is None else late + term
    late = late.astype(bf16)
    piece = late.shape[0] // blocks
    extra = early_ref.shape[0] // blocks
    for at in range(blocks):
        message_ref[at, pl.ds(0, extra), :] = early_ref[pl.ds(at * extra, extra), :]
        message_ref[at, pl.ds(extra, piece), :] = late[at * piece : (at + 1) * piece]


def meet(turn, arriving, nodes, early):
    blocks, share, width = arriving.shape
    own, deep = nodes[0].shape
    height = (early.shape[0] + deep) // blocks
    return pl.pallas_call(
        meet_body,
        grid_spec=pltpu.PrefetchScalarGridSpec(
            num_scalar_prefetch=1,
            grid=(1,),
            in_specs=[whole(*arriving.shape), whole(*early.shape)] + [whole(own, deep)] * len(nodes),
            out_specs=[whole(share, width), whole(blocks, height, width)],
        ),
        out_shape=[
            jax.ShapeDtypeStruct((share, width), jnp.bfloat16),
            jax.ShapeDtypeStruct((blocks, height, width), jnp.bfloat16),
        ],
        compiler_params=pltpu.CompilerParams(vmem_limit_bytes=24 * 1024 * 1024),
        cost_estimate=pl.CostEstimate(
            flops=2 * share * deep * width, bytes_accessed=4 * 2**20, transcendentals=0
        ),
        name="meet",
    )(turn, arriving, in_hbm(early), *map(in_hbm, nodes))


def finish_body(node_scale, edge_scale, sums_ref, src_ref, dst_ref, one_ref, two_ref, three_ref, node_ref):
    blocks, height, width = sums_ref.shape
    deep = src_ref.shape[0]
    piece = deep // blocks
    extra = height - piece
    for at in range(blocks):
        late = sums_ref[at, pl.ds(extra, piece), :].astype(jnp.float32)
        dst_ref[pl.ds(at * piece, piece), :] = late * node_scale
    squares = (one_ref, two_ref, three_ref)
    for low in range(0, 2 * deep + 3 * width, piece):
        at, place = low // extra, low % extra
        value = sums_ref[at, pl.ds(place, piece), :].astype(jnp.float32)
        if low < deep:
            src_ref[pl.ds(low, piece), :] = value * node_scale
        elif low < deep + 3 * width:
            which, row = (low - deep) // width, (low - deep) % width
            squares[which][pl.ds(row, piece), :] = value * edge_scale
        else:
            slab, row = (low - deep - 3 * width) // width, (low - deep - 3 * width) % width
            node_ref[pl.ds(row, piece), pl.ds(slab * width, width)] = value * node_scale


def finish(sums, deep, node_scale, edge_scale):
    width = sums.shape[2]
    shapes = [(deep, width)] * 2 + [(width, width)] * 3 + [(width, deep)]
    return pl.pallas_call(
        functools.partial(finish_body, node_scale, edge_scale),
        grid=(1,),
        in_specs=[pl.BlockSpec(memory_space=pltpu.VMEM)],
        out_specs=[whole(*shape) for shape in shapes],
        out_shape=[pltpu.HBM(shape, jnp.float32) for shape in shapes],
        compiler_params=pltpu.CompilerParams(vmem_limit_bytes=8 * 1024 * 1024),
        name="finish",
    )(sums)


def shards(
    node_in,
    edge_in,
    neighbours,
    edge_mask,
    w_src,
    w_dst,
    w_edge_one,
    w_edge_two,
    w_edge_three,
    w_node,
    node_cot,
    edge_cot,
):
    row_count, nbr_count, width = edge_in.shape
    deep = node_in.shape[1]
    bf16, f32 = jnp.bfloat16, jnp.float32
    long, tall, wide = lax.axis_size("z"), lax.axis_size("y"), lax.axis_size("x")
    blocks = wide * tall
    total = blocks * long * row_count
    node_scale = 1.0 / math.sqrt(total)
    edge_scale = 1.0 / math.sqrt(total * nbr_count)

    column = exchange(project(node_in, w_dst, long), RING)
    own_row, rest = neighbours % row_count, neighbours // row_count
    at_x, rest = rest % wide, rest // wide
    places = ((at_x * (tall * long) + rest) * row_count + own_row).reshape(-1)
    column, places, node_late = lax.optimization_barrier((column, places, node_in))
    table = spread(column.reshape(-1, width), PLANE).reshape(total, width)
    turns = [[(at, (at + shift) % long) for at in range(long)] for shift in range(long)]
    nodes = [node_in] + [lax.ppermute(node_late, "z", pairs) for pairs in turns[1 : long // 2]]
    edges = edge_in.reshape(row_count * nbr_count, width)
    cots = edge_cot.reshape(row_count * nbr_count, width)
    base, up = edge_prep(
        edges, cots, edge_mask, node_in, node_cot, w_src, w_edge_one, w_edge_three, w_node
    )
    half = long // 2
    table, base, up, *nodes = lax.optimization_barrier((table, base, up, *nodes))
    *chain, message = edge_chain(places, table, base, up, w_edge_two)
    *chain, message, node_late = lax.optimization_barrier((*chain, message, node_late))
    nodes += [lax.ppermute(node_late, "z", pairs) for pairs in turns[half:]]
    arriving = exchange(message.reshape(blocks, -1, width), PLANE)
    extra = -(-(2 * deep + 3 * width) // (blocks * 16)) * 16
    edge_out, grad_edge, early, node_out, grad_node = edge_side(
        edges,
        cots,
        edge_mask,
        chain,
        node_in,
        node_cot,
        w_src,
        w_edge_one,
        w_edge_three,
        w_node,
        blocks * extra,
    )
    arriving, early, *nodes = lax.optimization_barrier((arriving, early, *nodes))
    turn = jnp.full((1,), lax.axis_index("z"), jnp.int32)
    partial, message = meet(turn, arriving, nodes, early)
    weights = sum_first(exchange(message, PLANE)).astype(bf16)
    weights = jnp.broadcast_to(weights[None], (long, *weights.shape))
    packed = jnp.concatenate([partial.reshape(long, row_count, width), weights], axis=1)
    own = sum_first(exchange(packed, RING)).astype(bf16)
    grad_node = (grad_node + dot_turned(own[:row_count], w_dst)).astype(bf16)
    weights = finish(spread(own[row_count:], PLANE), deep, node_scale, edge_scale)
    return (
        node_out,
        edge_out.reshape(edge_in.shape),
        grad_node,
        grad_edge.reshape(edge_in.shape),
        *weights,
    )


def solution(mesh):
    shape = mesh.shape
    outer = shape["node"]
    inner = outer
    devices = mesh.devices.reshape(shape["cplx"], outer, shape["edge"] // inner, inner)
    mesh = Mesh(devices, ("cplx", *ALL))
    in_specs = (
        P(("cplx", *ALL), None),
        P(("cplx", *ALL), None, None),
        P(("cplx", *ALL), None),
        P(("cplx", *ALL), None),
        P(),
        P(),
        P(),
        P(),
        P(),
        P(),
        P(("cplx", *ALL), None),
        P(("cplx", *ALL), None, None),
    )
    out_specs = (
        P(("cplx", *ALL), None),
        P(("cplx", *ALL), None, None),
        P(("cplx", *ALL), None),
        P(("cplx", *ALL), None, None),
        P("cplx", None),
        P("cplx", None),
        P("cplx", None),
        P("cplx", None),
        P("cplx", None),
        P("cplx", None),
    )
    return jax.shard_map(shards, mesh=mesh, in_specs=in_specs, out_specs=out_specs, check_vma=False)
```

```python
import functools
import math

import jax
import jax.numpy as jnp
from jax import lax
from jax.experimental import pallas as pl
from jax.experimental.pallas import tpu as pltpu
from jax.sharding import Mesh
from jax.sharding import PartitionSpec as P

RING = ("z",)
PLANE = ("x", "y")
ALL = ("y", "z", "x")
SUMS = 4
BLOCK = 1024
CHUNKS = 8
SIDE_BLOCK = 1024
PIECE = 512


def exchange(value, axes):
    return lax.all_to_all(value, axes, 0, 0, tiled=True)


def spread(value, axes):
    count = math.prod(lax.axis_size(axis) for axis in axes)
    return exchange(jnp.broadcast_to(value[None], (count, *value.shape)), axes)


def sum_first(value):
    return jnp.sum(value.astype(jnp.float32), axis=0)


def sigmoid(value):
    return 0.5 * jnp.tanh(0.5 * value) + 0.5


def deriv(value, sigma_val):
    return sigma_val * (1.0 + value * (1.0 - sigma_val))


def dot(left, right):
    return jnp.dot(left, right, preferred_element_type=jnp.float32)


def dot_turned(left, right):
    return lax.dot_general(
        left, right, (((1,), (1,)), ((), ())), preferred_element_type=jnp.float32
    )


def dot_rows(left, right):
    return lax.dot_general(
        left, right, (((0,), (0,)), ((), ())), preferred_element_type=jnp.float32
    )


def rows_of(values, count):
    width = values.shape[1]
    rows = [jnp.broadcast_to(values[j : j + 1, :], (count, width)) for j in range(values.shape[0])]
    return jnp.concatenate(rows, axis=0)


def mask_of(mask, width):
    turned = mask.astype(jnp.float32).T
    count = turned.shape[0]
    columns = [jnp.broadcast_to(turned[:, j : j + 1], (count, width)) for j in range(mask.shape[0])]
    return jnp.concatenate(columns, axis=0)


def project_body(node_ref, weight_ref, out_ref):
    value = dot(node_ref[...], weight_ref[...]).astype(jnp.bfloat16)
    for at in range(out_ref.shape[0]):
        out_ref[at] = value


def whole(*shape):
    return pl.BlockSpec(shape, lambda i, *places: (0,) * len(shape))


def in_hbm(value):
    return pltpu.with_memory_space_constraint(value, pltpu.HBM)


def project(node_in, weight, count):
    nodes, width = node_in.shape[0], weight.shape[1]
    return pl.pallas_call(
        project_body,
        grid=(1,),
        in_specs=[whole(*node_in.shape), whole(*weight.shape)],
        out_specs=whole(count, nodes, width),
        out_shape=pltpu.HBM((count, nodes, width), jnp.bfloat16),
        compiler_params=pltpu.CompilerParams(vmem_limit_bytes=8 * 1024 * 1024),
        name="project",
    )(in_hbm(node_in), in_hbm(weight))


def prep_body(
    agg_scale,
    edge_ref,
    cot_ref,
    mask_ref,
    node_ref,
    node_cot_ref,
    w_src_ref,
    one_ref,
    three_ref,
    w_node_ref,
    base_ref,
    up_ref,
    src_proj,
    grad_agg,
):
    step = pl.program_id(0)
    groups, nbrs = mask_ref.shape
    width = edge_ref.shape[1]
    bf16, f32 = jnp.bfloat16, jnp.float32

    @pl.when(step == 0)
    def _():
        src_proj[...] = dot(node_ref[...], w_src_ref[...]).astype(bf16).astype(f32)
        grad_agg[...] = dot_turned(node_cot_ref[...], w_node_ref[...]) * agg_scale

    row = pl.multiple_of(step * groups, groups)
    masked = mask_of(mask_ref[...], width)
    agg_rows = rows_of(grad_agg[pl.ds(row, groups), :], nbrs)
    grad_upd = (masked * (cot_ref[...].astype(f32) + masked * agg_rows)).astype(bf16)
    up_ref[...] = dot_turned(grad_upd, three_ref[...])
    src_rows = rows_of(src_proj[pl.ds(row, groups), :], nbrs)
    base_ref[...] = dot(edge_ref[...], one_ref[...]) + src_rows


def edge_prep(edges, cots, mask, node_in, node_cot, w_src, w_one, w_three, w_node):
    total, width = edges.shape
    nodes, nbrs = mask.shape
    deep = node_in.shape[1]
    rest = (edges, cots, mask, node_in, node_cot, w_src, w_one, w_three, w_node)
    rows = pl.BlockSpec((SIDE_BLOCK, width), lambda i: (i, 0))
    masks = pl.BlockSpec((SIDE_BLOCK // nbrs, nbrs), lambda i: (i, 0))
    square = whole(width, width)
    small = pltpu.VMEM((nodes, width), jnp.float32)
    return pl.pallas_call(
        functools.partial(prep_body, 1.0 / math.sqrt(nbrs)),
        grid=(total // SIDE_BLOCK,),
        in_specs=[rows, rows, masks, whole(nodes, deep), whole(nodes, deep), whole(deep, width)]
        + [square, square, whole(width, deep)],
        out_specs=[rows, rows],
        scratch_shapes=[small, small],
        out_shape=[pltpu.HBM((total, width), jnp.float32)] * 2,
        compiler_params=pltpu.CompilerParams(vmem_limit_bytes=24 * 1024 * 1024),
        cost_estimate=pl.CostEstimate(
            flops=4 * total * width * width, bytes_accessed=12 * 2**20, transcendentals=0
        ),
        name="edge_prep",
    )(*map(in_hbm, rest))


def chain_body(
    place_ref,
    table_ref,
    base_ref,
    up_ref,
    two_ref,
    act_one_ref,
    act_two_ref,
    grad_two_ref,
    grad_one_ref,
    message_ref,
    table,
    *held,
):
    step = pl.program_id(0)
    count, width = table.shape
    block = base_ref.shape[0]
    chunk = block // CHUNKS
    sums, pulled, grads = held[:SUMS], held[SUMS : SUMS + CHUNKS], held[SUMS + CHUNKS :]
    bf16, f32 = jnp.bfloat16, jnp.float32

    @pl.when(step == 0)
    def _():
        def fill(at, carry):
            rows = pl.ds(pl.multiple_of(at * PIECE, PIECE), PIECE)
            table[rows, :] = table_ref[rows, :].astype(f32)
            for one in sums:
                one[rows, :] = jnp.zeros((PIECE, width), f32)
            return carry

        lax.fori_loop(0, count // PIECE, fill, 0)

    first = step * block

    def pull(at):
        for k in range(chunk):
            place = place_ref[first + at * chunk + k]
            pulled[at][pl.ds(k, 1), :] = table[pl.ds(place, 1), :]

    def push(at):
        for k in range(chunk):
            one = sums[k % SUMS]
            place = pl.ds(place_ref[first + at * chunk + k], 1)
            one[place, :] += grads[at][pl.ds(k, 1), :]

    def work(at):
        span = pl.ds(at * chunk, chunk)
        pre_one = base_ref[span, :] + pulled[at][...]
        sigma_one = sigmoid(pre_one)
        act_one = (pre_one * sigma_one).astype(bf16)
        act_one_ref[span, :] = act_one
        pre_two = dot(act_one, two_ref[...])
        sigma_two = sigmoid(pre_two)
        act_two_ref[span, :] = (pre_two * sigma_two).astype(bf16)
        grad_two = (up_ref[span, :] * deriv(pre_two, sigma_two)).astype(bf16)
        grad_two_ref[span, :] = grad_two
        grad_one = (dot_turned(grad_two, two_ref[...]) * deriv(pre_one, sigma_one)).astype(bf16)
        grad_one_ref[span, :] = grad_one
        grads[at][...] = grad_one.astype(f32)

    pull(0)
    for at in range(CHUNKS):
        if at + 1 < CHUNKS:
            pull(at + 1)
        work(at)
        if at > 0:
            push(at - 1)
    push(CHUNKS - 1)

    @pl.when(step == pl.num_programs(0) - 1)
    def _():
        def merge(at, carry):
            rows = pl.ds(pl.multiple_of(at * PIECE, PIECE), PIECE)
            value = sums[0][rows, :]
            for one in sums[1:]:
                value = value + one[rows, :]
            message_ref[rows, :] = value.astype(bf16)
            return carry

        lax.fori_loop(0, count // PIECE, merge, 0)


def edge_chain(places, table, base, up, w_two):
    count, width = table.shape
    total = places.shape[0]
    f32, bf16 = jnp.float32, jnp.bfloat16
    rows = pl.BlockSpec((BLOCK, width), lambda i, places: (i, 0))
    held = pltpu.VMEM((count, width), f32)
    part = pltpu.VMEM((BLOCK // CHUNKS, width), f32)
    return pl.pallas_call(
        chain_body,
        grid_spec=pltpu.PrefetchScalarGridSpec(
            num_scalar_prefetch=1,
            grid=(total // BLOCK,),
            in_specs=[pl.BlockSpec(memory_space=pltpu.VMEM), rows, rows, whole(width, width)],
            out_specs=[rows] * 4 + [whole(count, width)],
            scratch_shapes=[held] + [held] * SUMS + [part] * (2 * CHUNKS),
        ),
        out_shape=[pltpu.HBM((total, width), bf16)] * 4 + [pltpu.HBM((count, width), bf16)],
        compiler_params=pltpu.CompilerParams(vmem_limit_bytes=44 * 1024 * 1024),
        cost_estimate=pl.CostEstimate(
            flops=8 * total * width * width, bytes_accessed=12 * 2**20, transcendentals=0
        ),
        name="edge_chain",
    )(places, table, in_hbm(base), in_hbm(up), in_hbm(w_two))


def side_body(
    agg_scale,
    edge_ref,
    cot_ref,
    mask_ref,
    act_one_ref,
    act_two_ref,
    grad_two_ref,
    grad_one_ref,
    node_ref,
    node_cot_ref,
    w_src_ref,
    one_ref,
    three_ref,
    w_node_ref,
    edge_out_ref,
    grad_edge_ref,
    early_ref,
    node_out_ref,
    grad_node_ref,
    grad_agg,
    aggregate,
    grad_src,
    terms,
):
    step = pl.program_id(0)
    groups, nbrs = mask_ref.shape
    width = edge_ref.shape[1]
    deep = node_ref.shape[1]
    bf16, f32 = jnp.bfloat16, jnp.float32

    @pl.when(step == 0)
    def _():
        terms[...] = jnp.zeros(terms.shape, f32)
        grad_agg[...] = dot_turned(node_cot_ref[...], w_node_ref[...]) * agg_scale

    row = pl.multiple_of(step * groups, groups)
    masked = mask_of(mask_ref[...], width)
    grad_new = cot_ref[...].astype(f32) + masked * rows_of(grad_agg[pl.ds(row, groups), :], nbrs)
    grad_upd = (masked * grad_new).astype(bf16)
    grad_one = grad_one_ref[...]
    grad_edge_ref[...] = (grad_new + dot_turned(grad_one, one_ref[...])).astype(bf16)
    edges = edge_ref[...]
    act_two = act_two_ref[...]
    edge_new = edges.astype(f32) + masked * dot(act_two, three_ref[...])
    edge_out_ref[...] = edge_new.astype(bf16)
    kept = masked * edge_new
    grad_wide = grad_one.astype(f32)
    added, grouped = [], []
    for j in range(groups):
        part = slice(j * nbrs, (j + 1) * nbrs)
        added.append(jnp.sum(kept[part], axis=0, keepdims=True))
        grouped.append(jnp.sum(grad_wide[part], axis=0, keepdims=True))
    aggregate[pl.ds(row, groups), :] = jnp.concatenate(added, axis=0) * agg_scale
    grad_src[pl.ds(row, groups), :] = jnp.concatenate(grouped, axis=0)
    pairs = ((edges, grad_one), (act_one_ref[...], grad_two_ref[...]), (act_two, grad_upd))
    for at, (left, right) in enumerate(pairs):
        terms[pl.ds(at * width, width), :] += dot_rows(left, right)

    @pl.when(step == pl.num_programs(0) - 1)
    def _():
        agg = aggregate[...].astype(bf16)
        node_out_ref[...] = (node_ref[...].astype(f32) + dot(agg, w_node_ref[...])).astype(bf16)
        src = grad_src[...].astype(bf16)
        grad_node_ref[...] = node_cot_ref[...].astype(f32) + dot_turned(src, w_src_ref[...])
        early_ref[pl.ds(0, deep), :] = dot_rows(node_ref[...], src).astype(bf16)
        early_ref[pl.ds(deep, 3 * width), :] = terms[...].astype(bf16)
        low = deep + 3 * width
        for at in range(0, deep, width):
            slab = dot_rows(agg, node_cot_ref[:, pl.ds(at, width)])
            early_ref[pl.ds(low + at, width), :] = slab.astype(bf16)
        low = low + deep
        rest = early_ref.shape[0] - low
        early_ref[pl.ds(low, rest), :] = jnp.zeros((rest, width), bf16)


def edge_side(
    edges, cots, mask, chain, node_in, node_cot, w_src, w_one, w_three, w_node, early_rows
):
    total, width = edges.shape
    nodes, nbrs = mask.shape
    rest = tuple(map(in_hbm, (node_in, node_cot, w_src, w_one, w_three, w_node)))
    deep = node_in.shape[1]
    f32, bf16 = jnp.float32, jnp.bfloat16
    rows = pl.BlockSpec((SIDE_BLOCK, width), lambda i: (i, 0))
    masks = pl.BlockSpec((SIDE_BLOCK // nbrs, nbrs), lambda i: (i, 0))
    square = whole(width, width)
    small = pltpu.VMEM((nodes, width), f32)
    return pl.pallas_call(
        functools.partial(side_body, 1.0 / math.sqrt(nbrs)),
        grid=(total // SIDE_BLOCK,),
        in_specs=[rows, rows, masks] + [rows] * 4 + [whole(nodes, deep), whole(nodes, deep)]
        + [whole(deep, width), square, square, whole(width, deep)],
        out_specs=[rows, rows, whole(early_rows, width), whole(nodes, deep), whole(nodes, deep)],
        scratch_shapes=[small, small, small, pltpu.VMEM((3 * width, width), f32)],
        out_shape=[pltpu.HBM((total, width), bf16)] * 2
        + [pltpu.HBM((early_rows, width), bf16)]
        + [pltpu.HBM((nodes, deep), bf16), pltpu.HBM((nodes, deep), f32)],
        compiler_params=pltpu.CompilerParams(vmem_limit_bytes=24 * 1024 * 1024),
        cost_estimate=pl.CostEstimate(
            flops=10 * total * width * width, bytes_accessed=24 * 2**20, transcendentals=0
        ),
        name="edge_side",
    )(*map(in_hbm, (edges, cots)), in_hbm(mask), *map(in_hbm, chain), *rest)


def meet_body(turn_ref, arriving_ref, early_ref, *rest):
    *node_refs, partial_ref, message_ref = rest
    blocks, share, width = arriving_ref.shape
    count = len(node_refs)
    own = share // count
    bf16, f32 = jnp.bfloat16, jnp.float32
    value = arriving_ref[0].astype(f32)
    for at in range(1, blocks):
        value = value + arriving_ref[at].astype(f32)
    partial_ref[...] = value.astype(bf16)
    late = None
    for shift, node_ref in enumerate(node_refs):
        place = lax.rem(turn_ref[0] + (count - shift), count)
        rows = pl.ds(pl.multiple_of(place * own, own), own)
        term = dot_rows(node_ref[...], partial_ref[rows, :])
        late = term if late is None else late + term
    late = late.astype(bf16)
    piece = late.shape[0] // blocks
    extra = early_ref.shape[0] // blocks
    for at in range(blocks):
        message_ref[at, pl.ds(0, extra), :] = early_ref[pl.ds(at * extra, extra), :]
        message_ref[at, pl.ds(extra, piece), :] = late[at * piece : (at + 1) * piece]


def meet(turn, arriving, nodes, early):
    blocks, share, width = arriving.shape
    own, deep = nodes[0].shape
    height = (early.shape[0] + deep) // blocks
    return pl.pallas_call(
        meet_body,
        grid_spec=pltpu.PrefetchScalarGridSpec(
            num_scalar_prefetch=1,
            grid=(1,),
            in_specs=[pl.BlockSpec(memory_space=pltpu.VMEM), whole(*early.shape)]
            + [whole(own, deep)] * len(nodes),
            out_specs=[whole(share, width), whole(blocks, height, width)],
        ),
        out_shape=[
            jax.ShapeDtypeStruct((share, width), jnp.bfloat16),
            jax.ShapeDtypeStruct((blocks, height, width), jnp.bfloat16),
        ],
        compiler_params=pltpu.CompilerParams(vmem_limit_bytes=16 * 1024 * 1024),
        cost_estimate=pl.CostEstimate(
            flops=2 * share * deep * width, bytes_accessed=4 * 2**20, transcendentals=0
        ),
        name="meet",
    )(turn, arriving, in_hbm(early), *map(in_hbm, nodes))


def finish_body(
    node_scale,
    edge_scale,
    sums_ref,
    grad_dst_ref,
    base_ref,
    w_dst_ref,
    grad_node_ref,
    src_ref,
    dst_ref,
    one_ref,
    two_ref,
    three_ref,
    node_ref,
):
    blocks, height, width = sums_ref.shape
    deep = src_ref.shape[0]
    piece = deep // blocks
    extra = height - piece
    value = base_ref[...] + dot_turned(grad_dst_ref[...], w_dst_ref[...])
    grad_node_ref[...] = value.astype(jnp.bfloat16)
    for at in range(blocks):
        late = sums_ref[at, pl.ds(extra, piece), :].astype(jnp.float32)
        dst_ref[pl.ds(at * piece, piece), :] = late * node_scale
    squares = (one_ref, two_ref, three_ref)
    for low in range(0, 2 * deep + 3 * width, piece):
        at, place = low // extra, low % extra
        value = sums_ref[at, pl.ds(place, piece), :].astype(jnp.float32)
        if low < deep:
            src_ref[pl.ds(low, piece), :] = value * node_scale
        elif low < deep + 3 * width:
            which, row = (low - deep) // width, (low - deep) % width
            squares[which][pl.ds(row, piece), :] = value * edge_scale
        else:
            slab, row = (low - deep - 3 * width) // width, (low - deep - 3 * width) % width
            node_ref[pl.ds(row, piece), pl.ds(slab * width, width)] = value * node_scale


def finish(sums, own, base, w_dst, node_scale, edge_scale):
    deep, width = w_dst.shape
    shapes = [(deep, width)] * 2 + [(width, width)] * 3 + [(width, deep)]
    return pl.pallas_call(
        functools.partial(finish_body, node_scale, edge_scale),
        grid=(1,),
        in_specs=[pl.BlockSpec(memory_space=pltpu.VMEM), whole(base.shape[0], width)]
        + [whole(*base.shape), whole(deep, width)],
        out_specs=[whole(*base.shape)] + [whole(*shape) for shape in shapes],
        out_shape=[pltpu.HBM(base.shape, jnp.bfloat16)]
        + [pltpu.HBM(shape, jnp.float32) for shape in shapes],
        compiler_params=pltpu.CompilerParams(vmem_limit_bytes=8 * 1024 * 1024),
        name="finish",
    )(sums, own, in_hbm(base), in_hbm(w_dst))


def shards(
    node_in,
    edge_in,
    neighbours,
    edge_mask,
    w_src,
    w_dst,
    w_edge_one,
    w_edge_two,
    w_edge_three,
    w_node,
    node_cot,
    edge_cot,
):
    row_count, nbr_count, width = edge_in.shape
    deep = node_in.shape[1]
    bf16, f32 = jnp.bfloat16, jnp.float32
    long, tall, wide = lax.axis_size("z"), lax.axis_size("y"), lax.axis_size("x")
    blocks = wide * tall
    total = blocks * long * row_count
    node_scale = 1.0 / math.sqrt(total)
    edge_scale = 1.0 / math.sqrt(total * nbr_count)

    column = exchange(project(node_in, w_dst, long), RING)
    own_row, rest = neighbours % row_count, neighbours // row_count
    at_x, rest = rest % wide, rest // wide
    places = ((at_x * (tall * long) + rest) * row_count + own_row).reshape(-1)
    column, places, node_late = lax.optimization_barrier((column, places, node_in))
    table = spread(column.reshape(-1, width), PLANE).reshape(total, width)
    turns = [[(at, (at + shift) % long) for at in range(long)] for shift in range(long)]
    nodes = [node_in] + [lax.ppermute(node_late, "z", pairs) for pairs in turns[1 : long // 2]]
    edges = edge_in.reshape(row_count * nbr_count, width)
    cots = edge_cot.reshape(row_count * nbr_count, width)
    base, up = edge_prep(
        edges, cots, edge_mask, node_in, node_cot, w_src, w_edge_one, w_edge_three, w_node
    )
    half = long // 2
    table, base, up, *nodes = lax.optimization_barrier((table, base, up, *nodes))
    *chain, message = edge_chain(places, table, base, up, w_edge_two)
    *chain, message, node_late = lax.optimization_barrier((*chain, message, node_late))
    nodes += [lax.ppermute(node_late, "z", pairs) for pairs in turns[half:]]
    arriving = exchange(message.reshape(blocks, -1, width), PLANE)
    extra = -(-(2 * deep + 3 * width) // (blocks * 16)) * 16
    edge_out, grad_edge, early, node_out, grad_node = edge_side(
        edges,
        cots,
        edge_mask,
        chain,
        node_in,
        node_cot,
        w_src,
        w_edge_one,
        w_edge_three,
        w_node,
        blocks * extra,
    )
    arriving, early, *nodes = lax.optimization_barrier((arriving, early, *nodes))
    turn = jnp.full((1,), lax.axis_index("z"), jnp.int32)
    partial, message = meet(turn, arriving, nodes, early)
    weights = sum_first(exchange(message, PLANE)).astype(bf16)
    weights = jnp.broadcast_to(weights[None], (long, *weights.shape))
    packed = jnp.concatenate([partial.reshape(long, row_count, width), weights], axis=1)
    own = sum_first(exchange(packed, RING)).astype(bf16)
    sums = spread(own[row_count:], PLANE)
    grad_node, *weights = finish(sums, own, grad_node, w_dst, node_scale, edge_scale)
    return (
        node_out,
        edge_out.reshape(edge_in.shape),
        grad_node,
        grad_edge.reshape(edge_in.shape),
        *weights,
    )


def solution(mesh):
    shape = mesh.shape
    outer = shape["node"]
    inner = outer
    devices = mesh.devices.reshape(shape["cplx"], outer, shape["edge"] // inner, inner)
    mesh = Mesh(devices, ("cplx", *ALL))
    in_specs = (
        P(("cplx", *ALL), None),
        P(("cplx", *ALL), None, None),
        P(("cplx", *ALL), None),
        P(("cplx", *ALL), None),
        P(),
        P(),
        P(),
        P(),
        P(),
        P(),
        P(("cplx", *ALL), None),
        P(("cplx", *ALL), None, None),
    )
    out_specs = (
        P(("cplx", *ALL), None),
        P(("cplx", *ALL), None, None),
        P(("cplx", *ALL), None),
        P(("cplx", *ALL), None, None),
        P("cplx", None),
        P("cplx", None),
        P("cplx", None),
        P("cplx", None),
        P("cplx", None),
        P("cplx", None),
    )
    return jax.shard_map(shards, mesh=mesh, in_specs=in_specs, out_specs=out_specs, check_vma=False)
```

```python
import functools
import math

import jax
import jax.numpy as jnp
from jax import lax
from jax.experimental import pallas as pl
from jax.experimental.pallas import tpu as pltpu
from jax.sharding import Mesh
from jax.sharding import PartitionSpec as P

RING = ("z",)
PLANE = ("x", "y")
ALL = ("y", "z", "x")
SUMS = 4
BLOCK = 1024
CHUNKS = 8
SIDE_BLOCK = 1024
PIECE = 512


def exchange(value, axes):
    return lax.all_to_all(value, axes, 0, 0, tiled=True)


def spread(value, axes):
    count = math.prod(lax.axis_size(axis) for axis in axes)
    return exchange(jnp.broadcast_to(value[None], (count, *value.shape)), axes)


def sum_first(value):
    return jnp.sum(value.astype(jnp.float32), axis=0)


def sigmoid(value):
    return 0.5 * jnp.tanh(0.5 * value) + 0.5


def deriv(value, sigma_val):
    return sigma_val * (1.0 + value * (1.0 - sigma_val))


def dot(left, right):
    return jnp.dot(left, right, preferred_element_type=jnp.float32)


def dot_turned(left, right):
    return lax.dot_general(
        left, right, (((1,), (1,)), ((), ())), preferred_element_type=jnp.float32
    )


def dot_rows(left, right):
    return lax.dot_general(
        left, right, (((0,), (0,)), ((), ())), preferred_element_type=jnp.float32
    )


def rows_of(values, count):
    width = values.shape[1]
    rows = [jnp.broadcast_to(values[j : j + 1, :], (count, width)) for j in range(values.shape[0])]
    return jnp.concatenate(rows, axis=0)


def mask_of(mask, width):
    turned = mask.astype(jnp.float32).T
    count = turned.shape[0]
    columns = [jnp.broadcast_to(turned[:, j : j + 1], (count, width)) for j in range(mask.shape[0])]
    return jnp.concatenate(columns, axis=0)


def project_body(node_ref, weight_ref, out_ref):
    value = dot(node_ref[...], weight_ref[...]).astype(jnp.bfloat16)
    for at in range(out_ref.shape[0]):
        out_ref[at] = value


def whole(*shape):
    return pl.BlockSpec(shape, lambda i, *places: (0,) * len(shape))


def in_hbm(value):
    return pltpu.with_memory_space_constraint(value, pltpu.HBM)


def project(node_in, weight, count):
    nodes, width = node_in.shape[0], weight.shape[1]
    return pl.pallas_call(
        project_body,
        grid=(1,),
        in_specs=[whole(*node_in.shape), whole(*weight.shape)],
        out_specs=whole(count, nodes, width),
        out_shape=pltpu.HBM((count, nodes, width), jnp.bfloat16),
        compiler_params=pltpu.CompilerParams(vmem_limit_bytes=8 * 1024 * 1024),
        name="project",
    )(in_hbm(node_in), in_hbm(weight))


def prep_body(
    agg_scale,
    edge_ref,
    cot_ref,
    mask_ref,
    node_ref,
    node_cot_ref,
    w_src_ref,
    one_ref,
    three_ref,
    w_node_ref,
    base_ref,
    up_ref,
    src_proj,
    grad_agg,
):
    step = pl.program_id(0)
    groups, nbrs = mask_ref.shape
    width = edge_ref.shape[1]
    bf16, f32 = jnp.bfloat16, jnp.float32

    @pl.when(step == 0)
    def _():
        src_proj[...] = dot(node_ref[...], w_src_ref[...]).astype(bf16).astype(f32)
        grad_agg[...] = dot_turned(node_cot_ref[...], w_node_ref[...]) * agg_scale

    row = pl.multiple_of(step * groups, groups)
    masked = mask_of(mask_ref[...], width)
    agg_rows = rows_of(grad_agg[pl.ds(row, groups), :], nbrs)
    grad_upd = (masked * (cot_ref[...].astype(f32) + masked * agg_rows)).astype(bf16)
    up_ref[...] = dot_turned(grad_upd, three_ref[...])
    src_rows = rows_of(src_proj[pl.ds(row, groups), :], nbrs)
    base_ref[...] = dot(edge_ref[...], one_ref[...]) + src_rows


def edge_prep(edges, cots, mask, node_in, node_cot, w_src, w_one, w_three, w_node):
    total, width = edges.shape
    nodes, nbrs = mask.shape
    deep = node_in.shape[1]
    rest = (edges, cots, mask, node_in, node_cot, w_src, w_one, w_three, w_node)
    rows = pl.BlockSpec((SIDE_BLOCK, width), lambda i: (i, 0))
    masks = pl.BlockSpec((SIDE_BLOCK // nbrs, nbrs), lambda i: (i, 0))
    square = whole(width, width)
    small = pltpu.VMEM((nodes, width), jnp.float32)
    return pl.pallas_call(
        functools.partial(prep_body, 1.0 / math.sqrt(nbrs)),
        grid=(total // SIDE_BLOCK,),
        in_specs=[rows, rows, masks, whole(nodes, deep), whole(nodes, deep), whole(deep, width)]
        + [square, square, whole(width, deep)],
        out_specs=[rows, rows],
        scratch_shapes=[small, small],
        out_shape=[pltpu.HBM((total, width), jnp.float32)] * 2,
        compiler_params=pltpu.CompilerParams(vmem_limit_bytes=24 * 1024 * 1024),
        cost_estimate=pl.CostEstimate(
            flops=4 * total * width * width, bytes_accessed=12 * 2**20, transcendentals=0
        ),
        name="edge_prep",
    )(*map(in_hbm, rest))


def chain_body(
    place_ref,
    table_ref,
    base_ref,
    up_ref,
    two_ref,
    act_one_ref,
    act_two_ref,
    grad_two_ref,
    grad_one_ref,
    message_ref,
    table,
    *held,
):
    step = pl.program_id(0)
    count, width = table.shape
    block = base_ref.shape[0]
    chunk = block // CHUNKS
    sums, pulled, grads = held[:SUMS], held[SUMS : SUMS + CHUNKS], held[SUMS + CHUNKS :]
    bf16, f32 = jnp.bfloat16, jnp.float32

    @pl.when(step == 0)
    def _():
        def fill(at, carry):
            rows = pl.ds(pl.multiple_of(at * PIECE, PIECE), PIECE)
            table[rows, :] = table_ref[rows, :].astype(f32)
            for one in sums:
                one[rows, :] = jnp.zeros((PIECE, width), f32)
            return carry

        lax.fori_loop(0, count // PIECE, fill, 0)

    first = step * block

    def pull(at):
        for k in range(chunk):
            place = place_ref[first + at * chunk + k]
            pulled[at][pl.ds(k, 1), :] = table[pl.ds(place, 1), :]

    def push(at):
        for k in range(chunk):
            one = sums[k % SUMS]
            place = pl.ds(place_ref[first + at * chunk + k], 1)
            one[place, :] += grads[at][pl.ds(k, 1), :]

    def work(at):
        span = pl.ds(at * chunk, chunk)
        pre_one = base_ref[span, :] + pulled[at][...]
        sigma_one = sigmoid(pre_one)
        act_one = (pre_one * sigma_one).astype(bf16)
        act_one_ref[span, :] = act_one
        pre_two = dot(act_one, two_ref[...])
        sigma_two = sigmoid(pre_two)
        act_two_ref[span, :] = (pre_two * sigma_two).astype(bf16)
        grad_two = (up_ref[span, :] * deriv(pre_two, sigma_two)).astype(bf16)
        grad_two_ref[span, :] = grad_two
        grad_one = (dot_turned(grad_two, two_ref[...]) * deriv(pre_one, sigma_one)).astype(bf16)
        grad_one_ref[span, :] = grad_one
        grads[at][...] = grad_one.astype(f32)

    pull(0)
    for at in range(CHUNKS):
        if at + 1 < CHUNKS:
            pull(at + 1)
        work(at)
        if at > 0:
            push(at - 1)
    push(CHUNKS - 1)

    @pl.when(step == pl.num_programs(0) - 1)
    def _():
        def merge(at, carry):
            rows = pl.ds(pl.multiple_of(at * PIECE, PIECE), PIECE)
            value = sums[0][rows, :]
            for one in sums[1:]:
                value = value + one[rows, :]
            message_ref[rows, :] = value.astype(bf16)
            return carry

        lax.fori_loop(0, count // PIECE, merge, 0)


def edge_chain(places, table, base, up, w_two):
    count, width = table.shape
    total = places.shape[0]
    f32, bf16 = jnp.float32, jnp.bfloat16
    rows = pl.BlockSpec((BLOCK, width), lambda i, places: (i, 0))
    held = pltpu.VMEM((count, width), f32)
    part = pltpu.VMEM((BLOCK // CHUNKS, width), f32)
    return pl.pallas_call(
        chain_body,
        grid_spec=pltpu.PrefetchScalarGridSpec(
            num_scalar_prefetch=1,
            grid=(total // BLOCK,),
            in_specs=[pl.BlockSpec(memory_space=pltpu.VMEM), rows, rows, whole(width, width)],
            out_specs=[rows] * 4 + [whole(count, width)],
            scratch_shapes=[held] + [held] * SUMS + [part] * (2 * CHUNKS),
        ),
        out_shape=[pltpu.HBM((total, width), bf16)] * 4 + [pltpu.HBM((count, width), bf16)],
        compiler_params=pltpu.CompilerParams(vmem_limit_bytes=44 * 1024 * 1024),
        cost_estimate=pl.CostEstimate(
            flops=8 * total * width * width, bytes_accessed=12 * 2**20, transcendentals=0
        ),
        name="edge_chain",
    )(places, table, in_hbm(base), in_hbm(up), in_hbm(w_two))


def side_body(
    agg_scale,
    edge_ref,
    cot_ref,
    mask_ref,
    act_one_ref,
    act_two_ref,
    grad_two_ref,
    grad_one_ref,
    node_ref,
    node_cot_ref,
    w_src_ref,
    one_ref,
    three_ref,
    w_node_ref,
    edge_out_ref,
    grad_edge_ref,
    early_ref,
    node_out_ref,
    grad_node_ref,
    grad_agg,
    aggregate,
    grad_src,
    terms,
):
    step = pl.program_id(0)
    groups, nbrs = mask_ref.shape
    width = edge_ref.shape[1]
    deep = node_ref.shape[1]
    bf16, f32 = jnp.bfloat16, jnp.float32

    @pl.when(step == 0)
    def _():
        terms[...] = jnp.zeros(terms.shape, f32)
        grad_agg[...] = dot_turned(node_cot_ref[...], w_node_ref[...]) * agg_scale

    row = pl.multiple_of(step * groups, groups)
    masked = mask_of(mask_ref[...], width)
    grad_new = cot_ref[...].astype(f32) + masked * rows_of(grad_agg[pl.ds(row, groups), :], nbrs)
    grad_upd = (masked * grad_new).astype(bf16)
    grad_one = grad_one_ref[...]
    grad_edge_ref[...] = (grad_new + dot_turned(grad_one, one_ref[...])).astype(bf16)
    edges = edge_ref[...]
    act_two = act_two_ref[...]
    edge_new = edges.astype(f32) + masked * dot(act_two, three_ref[...])
    edge_out_ref[...] = edge_new.astype(bf16)
    kept = masked * edge_new
    grad_wide = grad_one.astype(f32)
    added, grouped = [], []
    for j in range(groups):
        part = slice(j * nbrs, (j + 1) * nbrs)
        added.append(jnp.sum(kept[part], axis=0, keepdims=True))
        grouped.append(jnp.sum(grad_wide[part], axis=0, keepdims=True))
    aggregate[pl.ds(row, groups), :] = jnp.concatenate(added, axis=0) * agg_scale
    grad_src[pl.ds(row, groups), :] = jnp.concatenate(grouped, axis=0)
    pairs = ((edges, grad_one), (act_one_ref[...], grad_two_ref[...]), (act_two, grad_upd))
    for at, (left, right) in enumerate(pairs):
        terms[pl.ds(at * width, width), :] += dot_rows(left, right)

    @pl.when(step == pl.num_programs(0) - 1)
    def _():
        agg = aggregate[...].astype(bf16)
        node_out_ref[...] = (node_ref[...].astype(f32) + dot(agg, w_node_ref[...])).astype(bf16)
        src = grad_src[...].astype(bf16)
        grad_node_ref[...] = node_cot_ref[...].astype(f32) + dot_turned(src, w_src_ref[...])
        early_ref[pl.ds(0, deep), :] = dot_rows(node_ref[...], src).astype(bf16)
        early_ref[pl.ds(deep, 3 * width), :] = terms[...].astype(bf16)
        low = deep + 3 * width
        for at in range(0, deep, width):
            slab = dot_rows(agg, node_cot_ref[:, pl.ds(at, width)])
            early_ref[pl.ds(low + at, width), :] = slab.astype(bf16)
        low = low + deep
        rest = early_ref.shape[0] - low
        early_ref[pl.ds(low, rest), :] = jnp.zeros((rest, width), bf16)


def edge_side(
    edges, cots, mask, chain, node_in, node_cot, w_src, w_one, w_three, w_node, early_rows
):
    total, width = edges.shape
    nodes, nbrs = mask.shape
    rest = tuple(map(in_hbm, (node_in, node_cot, w_src, w_one, w_three, w_node)))
    deep = node_in.shape[1]
    f32, bf16 = jnp.float32, jnp.bfloat16
    rows = pl.BlockSpec((SIDE_BLOCK, width), lambda i: (i, 0))
    masks = pl.BlockSpec((SIDE_BLOCK // nbrs, nbrs), lambda i: (i, 0))
    square = whole(width, width)
    small = pltpu.VMEM((nodes, width), f32)
    return pl.pallas_call(
        functools.partial(side_body, 1.0 / math.sqrt(nbrs)),
        grid=(total // SIDE_BLOCK,),
        in_specs=[rows, rows, masks] + [rows] * 4 + [whole(nodes, deep), whole(nodes, deep)]
        + [whole(deep, width), square, square, whole(width, deep)],
        out_specs=[rows, rows, whole(early_rows, width), whole(nodes, deep), whole(nodes, deep)],
        scratch_shapes=[small, small, small, pltpu.VMEM((3 * width, width), f32)],
        out_shape=[pltpu.HBM((total, width), bf16)] * 2
        + [pltpu.HBM((early_rows, width), bf16)]
        + [pltpu.HBM((nodes, deep), bf16), pltpu.HBM((nodes, deep), f32)],
        compiler_params=pltpu.CompilerParams(vmem_limit_bytes=24 * 1024 * 1024),
        cost_estimate=pl.CostEstimate(
            flops=10 * total * width * width, bytes_accessed=24 * 2**20, transcendentals=0
        ),
        name="edge_side",
    )(*map(in_hbm, (edges, cots)), in_hbm(mask), *map(in_hbm, chain), *rest)


def meet_body(turn_ref, arriving_ref, early_ref, *rest):
    *node_refs, partial_ref, message_ref = rest
    blocks, share, width = arriving_ref.shape
    count = len(node_refs)
    own = share // count
    bf16, f32 = jnp.bfloat16, jnp.float32
    value = arriving_ref[0].astype(f32)
    for at in range(1, blocks):
        value = value + arriving_ref[at].astype(f32)
    partial_ref[...] = value.astype(bf16)
    terms = []
    for shift in range(count):
        place = lax.rem(turn_ref[0] + (count - shift), count)
        terms.append(partial_ref[pl.ds(pl.multiple_of(place * own, own), own), :])
    nodes = jnp.concatenate([node_ref[...] for node_ref in node_refs], axis=0)
    late = dot_rows(nodes, jnp.concatenate(terms, axis=0))
    late = late.astype(bf16)
    piece = late.shape[0] // blocks
    extra = early_ref.shape[0] // blocks
    for at in range(blocks):
        message_ref[at, pl.ds(0, extra), :] = early_ref[pl.ds(at * extra, extra), :]
        message_ref[at, pl.ds(extra, piece), :] = late[at * piece : (at + 1) * piece]


def meet(turn, arriving, nodes, early):
    blocks, share, width = arriving.shape
    own, deep = nodes[0].shape
    height = (early.shape[0] + deep) // blocks
    return pl.pallas_call(
        meet_body,
        grid_spec=pltpu.PrefetchScalarGridSpec(
            num_scalar_prefetch=1,
            grid=(1,),
            in_specs=[pl.BlockSpec(memory_space=pltpu.VMEM), whole(*early.shape)]
            + [whole(own, deep)] * len(nodes),
            out_specs=[whole(share, width), whole(blocks, height, width)],
        ),
        out_shape=[
            jax.ShapeDtypeStruct((share, width), jnp.bfloat16),
            jax.ShapeDtypeStruct((blocks, height, width), jnp.bfloat16),
        ],
        compiler_params=pltpu.CompilerParams(vmem_limit_bytes=16 * 1024 * 1024),
        cost_estimate=pl.CostEstimate(
            flops=2 * share * deep * width, bytes_accessed=4 * 2**20, transcendentals=0
        ),
        name="meet",
    )(turn, arriving, in_hbm(early), *map(in_hbm, nodes))


def finish_body(node_scale, edge_scale, sums_ref, src_ref, dst_ref, one_ref, two_ref, three_ref, node_ref):
    blocks, height, width = sums_ref.shape
    deep = src_ref.shape[0]
    piece = deep // blocks
    extra = height - piece
    for at in range(blocks):
        late = sums_ref[at, pl.ds(extra, piece), :].astype(jnp.float32)
        dst_ref[pl.ds(at * piece, piece), :] = late * node_scale
    squares = (one_ref, two_ref, three_ref)
    for low in range(0, 2 * deep + 3 * width, piece):
        at, place = low // extra, low % extra
        value = sums_ref[at, pl.ds(place, piece), :].astype(jnp.float32)
        if low < deep:
            src_ref[pl.ds(low, piece), :] = value * node_scale
        elif low < deep + 3 * width:
            which, row = (low - deep) // width, (low - deep) % width
            squares[which][pl.ds(row, piece), :] = value * edge_scale
        else:
            slab, row = (low - deep - 3 * width) // width, (low - deep - 3 * width) % width
            node_ref[pl.ds(row, piece), pl.ds(slab * width, width)] = value * node_scale


def finish(sums, deep, node_scale, edge_scale):
    width = sums.shape[2]
    shapes = [(deep, width)] * 2 + [(width, width)] * 3 + [(width, deep)]
    return pl.pallas_call(
        functools.partial(finish_body, node_scale, edge_scale),
        grid=(1,),
        in_specs=[pl.BlockSpec(memory_space=pltpu.VMEM)],
        out_specs=[whole(*shape) for shape in shapes],
        out_shape=[pltpu.HBM(shape, jnp.float32) for shape in shapes],
        compiler_params=pltpu.CompilerParams(vmem_limit_bytes=8 * 1024 * 1024),
        name="finish",
    )(sums)


def shards(
    node_in,
    edge_in,
    neighbours,
    edge_mask,
    w_src,
    w_dst,
    w_edge_one,
    w_edge_two,
    w_edge_three,
    w_node,
    node_cot,
    edge_cot,
):
    row_count, nbr_count, width = edge_in.shape
    deep = node_in.shape[1]
    bf16, f32 = jnp.bfloat16, jnp.float32
    long, tall, wide = lax.axis_size("z"), lax.axis_size("y"), lax.axis_size("x")
    blocks = wide * tall
    total = blocks * long * row_count
    node_scale = 1.0 / math.sqrt(total)
    edge_scale = 1.0 / math.sqrt(total * nbr_count)

    column = exchange(project(node_in, w_dst, long), RING)
    own_row, rest = neighbours % row_count, neighbours // row_count
    at_x, rest = rest % wide, rest // wide
    places = ((at_x * (tall * long) + rest) * row_count + own_row).reshape(-1)
    column, places, node_late = lax.optimization_barrier((column, places, node_in))
    table = spread(column.reshape(-1, width), PLANE).reshape(total, width)
    turns = [[(at, (at + shift) % long) for at in range(long)] for shift in range(long)]
    nodes = [node_in] + [lax.ppermute(node_late, "z", pairs) for pairs in turns[1 : long // 2]]
    edges = edge_in.reshape(row_count * nbr_count, width)
    cots = edge_cot.reshape(row_count * nbr_count, width)
    base, up = edge_prep(
        edges, cots, edge_mask, node_in, node_cot, w_src, w_edge_one, w_edge_three, w_node
    )
    half = long // 2
    table, base, up, *nodes = lax.optimization_barrier((table, base, up, *nodes))
    *chain, message = edge_chain(places, table, base, up, w_edge_two)
    *chain, message, node_late = lax.optimization_barrier((*chain, message, node_late))
    nodes += [lax.ppermute(node_late, "z", pairs) for pairs in turns[half:]]
    arriving = exchange(message.reshape(blocks, -1, width), PLANE)
    extra = -(-(2 * deep + 3 * width) // (blocks * 16)) * 16
    edge_out, grad_edge, early, node_out, grad_node = edge_side(
        edges,
        cots,
        edge_mask,
        chain,
        node_in,
        node_cot,
        w_src,
        w_edge_one,
        w_edge_three,
        w_node,
        blocks * extra,
    )
    arriving, early, *nodes = lax.optimization_barrier((arriving, early, *nodes))
    turn = jnp.full((1,), lax.axis_index("z"), jnp.int32)
    partial, message = meet(turn, arriving, nodes, early)
    weights = sum_first(exchange(message, PLANE)).astype(bf16)
    weights = jnp.broadcast_to(weights[None], (long, *weights.shape))
    packed = jnp.concatenate([partial.reshape(long, row_count, width), weights], axis=1)
    own = sum_first(exchange(packed, RING)).astype(bf16)
    grad_node = (grad_node + dot_turned(own[:row_count], w_dst)).astype(bf16)
    weights = finish(spread(own[row_count:], PLANE), deep, node_scale, edge_scale)
    return (
        node_out,
        edge_out.reshape(edge_in.shape),
        grad_node,
        grad_edge.reshape(edge_in.shape),
        *weights,
    )


def solution(mesh):
    shape = mesh.shape
    outer = shape["node"]
    inner = outer
    devices = mesh.devices.reshape(shape["cplx"], outer, shape["edge"] // inner, inner)
    mesh = Mesh(devices, ("cplx", *ALL))
    in_specs = (
        P(("cplx", *ALL), None),
        P(("cplx", *ALL), None, None),
        P(("cplx", *ALL), None),
        P(("cplx", *ALL), None),
        P(),
        P(),
        P(),
        P(),
        P(),
        P(),
        P(("cplx", *ALL), None),
        P(("cplx", *ALL), None, None),
    )
    out_specs = (
        P(("cplx", *ALL), None),
        P(("cplx", *ALL), None, None),
        P(("cplx", *ALL), None),
        P(("cplx", *ALL), None, None),
        P("cplx", None),
        P("cplx", None),
        P("cplx", None),
        P("cplx", None),
        P("cplx", None),
        P("cplx", None),
    )
    return jax.shard_map(shards, mesh=mesh, in_specs=in_specs, out_specs=out_specs, check_vma=False)
```
